512 devices in a mesh: grp: 32 (over y, z_hi, core), leaf: 16 (over z_lo, x).
Axes of the slice: x: 4, y: 8, z: 8 (z_hi: 2, z_lo: 4; z = z_hi * 4 + z_lo), core: 2. Of those that a mesh axis runs over, the one named last changes fastest.
Arguments:
- vectors: bfloat16 [32, 2097152], P(None, ('grp', 'leaf')), may hold values from -6 to 6
- offsets: bfloat16 [3, 2097152], P(None, ('grp', 'leaf')), may hold values from 0 to 1
- near_list: int32 [8192, 16], P(('grp', 'leaf')), may hold values from 0 to 8191, as said below
- near_count: int32 [8192], P(('grp', 'leaf')), may hold values from 8 to 16, as said below
- leaf_basis: bfloat16 [8192, 64, 256], P(('grp', 'leaf')), may hold values from -0.375 to 0.375
- far_list: int32 [8192, 16], P(('grp', 'leaf')), may hold values from 0 to 8191, as said below
- far_count: int32 [8192], P(('grp', 'leaf')), may hold values from 0 to 16, as said below
- leaf_coupling: bfloat16 [8192, 16, 64, 64], P(('grp', 'leaf')), as said below
- transfer: bfloat16 [8192, 64, 64], P(('grp', 'leaf')), may hold values from -0.75 to 0.75
- group_list: int32 [32, 16], P('grp'), may hold values from 0 to 31, as said below
- group_count: int32 [32], P('grp'), may hold values from 8 to 16, as said below
- group_coupling: bfloat16 [32, 16, 64, 64], P('grp', 'leaf'), may hold values from -0.01171875 to 0.01171875
Outputs:
- applied: bfloat16 [32, 2097152], P(None, ('grp', 'leaf'))
The draws below stay inside these ranges and needn't reach their ends.
Inputs may be any that keep to these rules, and one draw needn't show every extreme that they name: `near_list`: the first near_count[l] entries of row l are distinct leaves of l's own group lying on l's device or on the devices just before and after it along leaf (16 consecutive leaves a device); the first entry is l itself and the remaining entries repeat l. `near_count`: the first leaf of every device has exactly 16. `far_list`: the first far_count[l] entries of row l are distinct leaves of l's own group other than l; the remaining entries repeat l. If leaf j stands in slot k < far_count[l] of row l, then l stands in some slot k2 < far_count[j] of row j. `far_count`: the first leaf of every group has exactly 16. If far_list[l, k] = j with k < far_count[l], and far_list[j, k2] = l with k2 < far_count[j], then leaf_coupling[j, k2] is the transpose of leaf_coupling[l, k]. `group_list`: the first group_count[g] entries of row g are distinct groups other than g; the remaining entries repeat g. `group_count`: group 0 has exactly 16.
All inputs are finite; a program needn't handle non-finite values.
Results may differ from the reference program's by a relative error of at most 0.005.
Values may be sent and summed in bfloat16 or wider, within the bound.
No kernel may reach another device: no remote copies, remote signals or barrier semaphores. Data moves between devices by JAX's collectives and lax.ppermute only.
A program may use at most 64 MiB of HBM per device.

```python
import jax
import jax.numpy as jnp
from jax import lax

LEAF_PTS = 256
RANK = 64
VECS = 32
LEAF_DEV = 16
NEAR = 16
GROUP_LEAVES = 256
FAR_SLOTS = 16
GROUP_SLOTS = 16
LEAVES = 8192
POINTS = 2097152
N_GRP = 32


def near_tables(key):
    leaf_ids = jnp.arange(LEAVES, dtype=jnp.int32)
    window = 3 * LEAF_DEV
    subkeys = jax.random.split(key, LEAVES)
    orders = jax.vmap(lambda subkey: jax.random.permutation(subkey, window))(subkeys).astype(jnp.int32)
    device_first = leaf_ids // LEAF_DEV * LEAF_DEV
    group_first = leaf_ids // GROUP_LEAVES * GROUP_LEAVES
    candidate = device_first[:, None] - LEAF_DEV + jnp.arange(window, dtype=jnp.int32)[None, :]
    inside = (candidate >= group_first[:, None]) & (candidate < group_first[:, None] + GROUP_LEAVES)
    scores = orders + window * (1 - inside.astype(jnp.int32))
    scores = jnp.where(candidate == leaf_ids[:, None], -1, scores)
    chosen_pos = jnp.argsort(scores, axis=1, stable=True)[:, :NEAR]
    chosen = jnp.take_along_axis(candidate, chosen_pos, axis=1)
    counts = jax.random.randint(jax.random.fold_in(key, 1), (LEAVES,), NEAR // 2, NEAR + 1).astype(jnp.int32)
    counts = jnp.where(leaf_ids % LEAF_DEV == 0, NEAR, counts)
    slot_ids = jnp.arange(NEAR, dtype=jnp.int32)
    chosen = jnp.where(slot_ids[None, :] < counts[:, None], chosen, leaf_ids[:, None])
    return (chosen.astype(jnp.int32), counts.astype(jnp.int32))


def far_group_tables(group_key):
    half_count = GROUP_LEAVES // 2
    strides = jax.random.permutation(jax.random.fold_in(group_key, 1), half_count)[:FAR_SLOTS].astype(jnp.int32) * 2 + 1
    local = jnp.arange(GROUP_LEAVES, dtype=jnp.int32)
    partner = (strides[None, :] - local[:, None]) % GROUP_LEAVES
    pair_low = jnp.minimum(local[:, None], partner)
    coins = jax.random.randint(jax.random.fold_in(group_key, 2), (GROUP_LEAVES, FAR_SLOTS), 0, 2).astype(jnp.int32)
    coin_pair = jnp.take_along_axis(coins, pair_low, axis=0)
    active = (coin_pair == 1) | (pair_low == 0)
    slot_ids = jnp.arange(FAR_SLOTS, dtype=jnp.int32)
    ranking = (1 - active.astype(jnp.int32)) * FAR_SLOTS + slot_ids[None, :]
    ordering = jnp.argsort(ranking, axis=1, stable=True)
    counts = jnp.sum(active.astype(jnp.int32), axis=1)
    partner_sorted = jnp.take_along_axis(partner, ordering, axis=1)
    entries = jnp.where(slot_ids[None, :] < counts[:, None], partner_sorted, local[:, None])
    scale = (2.0 / (RANK * FAR_SLOTS)) ** 0.5
    base = jax.random.normal(jax.random.fold_in(group_key, 3), (GROUP_LEAVES, FAR_SLOTS, RANK, RANK), jnp.float32) * scale
    mirrored = base[partner, slot_ids[None, :]]
    swapped = jnp.swapaxes(mirrored, -1, -2)
    coupling = jnp.where((local[:, None] < partner)[:, :, None, None], base, swapped)
    coupling = coupling[local[:, None], ordering]
    return (entries, counts, coupling)


def far_tables(key):
    groups = LEAVES // GROUP_LEAVES
    group_keys = jax.random.split(jax.random.fold_in(key, 2), groups)
    entries, counts, coupling = lax.map(far_group_tables, group_keys)
    group_base = (jnp.arange(groups, dtype=jnp.int32) * GROUP_LEAVES)[:, None, None]
    entries = (entries + group_base).reshape(LEAVES, FAR_SLOTS)
    return (entries.astype(jnp.int32), counts.reshape(LEAVES).astype(jnp.int32), coupling.reshape(LEAVES, FAR_SLOTS, RANK, RANK))


def group_tables(key):
    groups = LEAVES // GROUP_LEAVES
    group_keys = jax.random.split(jax.random.fold_in(key, 5), groups)
    picks = jax.vmap(lambda subkey: jax.random.permutation(subkey, groups - 1)[:GROUP_SLOTS])(group_keys).astype(jnp.int32)
    owners = jnp.arange(groups, dtype=jnp.int32)[:, None]
    entries = picks + (picks >= owners).astype(jnp.int32)
    counts = jax.random.randint(jax.random.fold_in(key, 6), (groups,), GROUP_SLOTS // 2, GROUP_SLOTS + 1).astype(jnp.int32)
    counts = counts.at[0].set(GROUP_SLOTS)
    slot_ids = jnp.arange(GROUP_SLOTS, dtype=jnp.int32)
    entries = jnp.where(slot_ids[None, :] < counts[:, None], entries, owners)
    return (entries.astype(jnp.int32), counts)


def draw_near_list(key, part):
    return near_tables(key)[0]


def draw_near_count(key, part):
    return near_tables(key)[1]


def draw_far_list(key, part):
    return far_tables(key)[0]


def draw_far_count(key, part):
    return far_tables(key)[1]


def draw_leaf_coupling(key, part):
    return far_tables(key)[2].astype(jnp.bfloat16)


def draw_group_list(key, part):
    return group_tables(key)[0]


def draw_group_count(key, part):
    return group_tables(key)[1]


def block_levels(key, extent, cuts, smallest, high):
    factor_of, own = 1.0, jax.random.fold_in(key, 6)
    for dim, shards_of in cuts:
        steps = jnp.exp(jax.random.uniform(jax.random.fold_in(own, dim), (shards_of,), jnp.float32, smallest / len(cuts), high / len(cuts)))
        factor_of = factor_of * jnp.repeat(steps, extent[dim] // shards_of).reshape([-1 if axis == dim else 1 for axis in range(len(extent))])
    return factor_of


def normal_values(key, dims, deviation, most, shards=(), kind=jnp.bfloat16):
    loudness = block_levels(key, dims, shards, -0.22, 0.18) if shards else 1.0
    values = jax.random.normal(key, dims, jnp.float32) * deviation * loudness
    return jnp.minimum(jnp.maximum(values, -most), most).astype(kind)


def setup_inputs(seed: int = 0) -> dict:
    key_list = jax.random.split(jax.random.key(seed), 13)
    vectors = normal_values(key_list[0], (VECS, POINTS), 1.0, 6.0, ((1, 512),))
    offsets = jnp.clip(1.0 * jax.random.uniform(key_list[1], (3, POINTS), jnp.float32) ** block_levels(key_list[1], (3, POINTS), ((1, 512),), -0.2, 0.2), 0.0, 1.0).astype(jnp.bfloat16)
    near_list = draw_near_list(jax.random.fold_in(key_list[12], 71), 0)
    near_count = draw_near_count(jax.random.fold_in(key_list[12], 71), 0)
    leaf_basis = normal_values(key_list[4], (LEAVES, RANK, LEAF_PTS), LEAF_PTS ** -0.5, 0.375, ((0, 512),))
    far_list = draw_far_list(jax.random.fold_in(key_list[12], 71), 0)
    far_count = draw_far_count(jax.random.fold_in(key_list[12], 71), 0)
    leaf_coupling = draw_leaf_coupling(jax.random.fold_in(key_list[12], 71), 0)
    transfer = normal_values(key_list[8], (LEAVES, RANK, RANK), RANK ** -0.5, 0.75, ((0, 512),))
    group_list = draw_group_list(jax.random.fold_in(key_list[12], 71), 0)
    group_count = draw_group_count(jax.random.fold_in(key_list[12], 71), 0)
    group_coupling = normal_values(key_list[11], (N_GRP, GROUP_SLOTS, RANK, RANK), (RANK * GROUP_SLOTS * GROUP_LEAVES) ** -0.5, 0.01171875, ((0, 32), (1, 16)))
    return {"vectors": vectors, "offsets": offsets, "near_list": near_list, "near_count": near_count, "leaf_basis": leaf_basis, "far_list": far_list, "far_count": far_count, "leaf_coupling": leaf_coupling, "transfer": transfer, "group_list": group_list, "group_count": group_count, "group_coupling": group_coupling}


inv_four_pi = 0.07957747154594767
soften = 0.01

def centres(leaf_ids):
    columns = []
    for axis_pos in range(3):
        summed = jnp.zeros_like(leaf_ids)
        for bit_pos in range(10):
            picked = jnp.bitwise_and(jnp.right_shift(leaf_ids, 3 * bit_pos + axis_pos), 1)
            summed = summed + jnp.left_shift(picked, bit_pos)
        columns.append(summed.astype(jnp.float32))
    return jnp.stack(columns)

def kernel_tile(source_pts, target_pts):
    squared = jnp.zeros((source_pts.shape[0], source_pts.shape[2], target_pts.shape[1]), jnp.float32)
    for axis_pos in range(3):
        spacing = source_pts[:, axis_pos, :, None] - target_pts[axis_pos][None, None, :]
        squared = squared + spacing * spacing
    return inv_four_pi * lax.rsqrt(squared + soften)

def reference(vectors, offsets, near_list, near_count, leaf_basis, far_list, far_count, leaf_coupling, transfer, group_list, group_count, group_coupling):
    groups = group_list.shape[0]
    leaf_vectors = vectors.reshape(VECS, LEAVES, LEAF_PTS)
    positions = offsets.astype(jnp.float32).reshape(3, LEAVES, LEAF_PTS) + centres(jnp.arange(LEAVES, dtype=jnp.int32))[:, :, None]
    near_slots = jnp.arange(NEAR, dtype=jnp.int32)

    def near_one(leaf_id):
        sources = near_list[leaf_id]
        active_slots = near_slots < near_count[leaf_id]
        source_pts = jnp.take(positions, sources, axis=1).transpose(1, 0, 2)
        target_pts = lax.dynamic_index_in_dim(positions, leaf_id, 1, keepdims=False)
        near_tile = jnp.where(active_slots[:, None, None], kernel_tile(source_pts, target_pts), 0.0)
        near_tile = lax.optimization_barrier(near_tile.astype(jnp.bfloat16))
        source_vectors = jnp.take(leaf_vectors, sources, axis=1)
        return jnp.einsum('vkb,kba->va', source_vectors.astype(jnp.float32), near_tile.astype(jnp.float32))
    near_field = lax.map(near_one, jnp.arange(LEAVES, dtype=jnp.int32))
    coeffs = jnp.einsum('vla,lra->lvr', leaf_vectors.astype(jnp.float32), leaf_basis.astype(jnp.float32))
    coeffs = lax.optimization_barrier(coeffs.astype(jnp.bfloat16))
    grouped = coeffs.reshape(groups, GROUP_LEAVES, VECS, RANK)
    far_slots = jnp.arange(FAR_SLOTS, dtype=jnp.int32)

    def far_group(group_id):
        group_first = group_id * GROUP_LEAVES
        source_rows = lax.dynamic_slice_in_dim(far_list, group_first, GROUP_LEAVES, 0) - group_first
        counts = lax.dynamic_slice_in_dim(far_count, group_first, GROUP_LEAVES, 0)
        couplings = lax.dynamic_slice_in_dim(leaf_coupling, group_first, GROUP_LEAVES, 0)
        members = lax.dynamic_index_in_dim(grouped, group_id, 0, keepdims=False)
        picked = jnp.take(members, source_rows, axis=0).astype(jnp.float32)
        active_slots = far_slots[None, :] < counts[:, None]
        picked = jnp.where(active_slots[:, :, None, None], picked, 0.0)
        return jnp.einsum('ikvs,ikrs->ivr', picked, couplings.astype(jnp.float32))
    far_field = lax.map(far_group, jnp.arange(groups, dtype=jnp.int32)).reshape(LEAVES, VECS, RANK)
    grouped_transfer = transfer.reshape(groups, GROUP_LEAVES, RANK, RANK).astype(jnp.float32)
    coarse = jnp.einsum('glvs,glsr->gvr', grouped.astype(jnp.float32), grouped_transfer)
    coarse = lax.optimization_barrier(coarse.astype(jnp.bfloat16))
    group_slots = jnp.arange(GROUP_SLOTS, dtype=jnp.int32)
    picked_groups = jnp.take(coarse, group_list, axis=0).astype(jnp.float32)
    picked_groups = jnp.where((group_slots[None, :] < group_count[:, None])[:, :, None, None], picked_groups, 0.0)
    coarse_out = jnp.einsum('gkvs,gkrs->gvr', picked_groups, group_coupling.astype(jnp.float32))
    coarse_out = lax.optimization_barrier(coarse_out.astype(jnp.bfloat16))
    downward = jnp.einsum('gvs,glrs->glvr', coarse_out.astype(jnp.float32), grouped_transfer).reshape(LEAVES, VECS, RANK)
    local_coeffs = lax.optimization_barrier((far_field + downward).astype(jnp.bfloat16))
    expanded = jnp.einsum('lvr,lra->vla', local_coeffs.astype(jnp.float32), leaf_basis.astype(jnp.float32))
    result = near_field.transpose(1, 0, 2) + expanded
    return result.reshape(VECS, POINTS).astype(jnp.bfloat16)
```

```python
import jax
import jax.numpy as jnp
from jax import lax
from jax.experimental import pallas as pl
from jax.experimental.pallas import tpu as pltpu
from jax.sharding import PartitionSpec as P

inv_four_pi = 0.07957747154594767
soften = 0.01
feature_depth = 128
slots_at_once = 4
id_bits = 5
vmem_bytes = 50 << 20

nt_dims = (((1,), (1,)), ((), ()))
nn_dims = (((1,), (0,)), ((), ()))
smem = pl.BlockSpec(memory_space=pltpu.SMEM)
vmem = pl.BlockSpec(memory_space=pltpu.VMEM)
params = pltpu.CompilerParams(vmem_limit_bytes=vmem_bytes)


def dot(left, right, dims):
    return lax.dot_general(left, right, dims, preferred_element_type=jnp.float32)


def pack(block):
    half = block.shape[0] // 2
    return jnp.concatenate([block[:half], block[half:]], axis=1)


def unpack(block):
    half = block.shape[1] // 2
    return jnp.concatenate([block[:, :half], block[:, half:]], axis=0)


def upward_kernel(vec_ref, off_ref, basis_ref, transfer_ref, group_ref, halo_ref, big_ref, small_ref):
    vecs, width = vec_ref.shape
    leaves = basis_ref.shape[0]
    points = width // leaves
    copies = big_ref.shape[0]
    rows = vecs // 2
    halo_ref[0:vecs, :] = vec_ref[...]
    halo_ref[vecs : vecs + off_ref.shape[0], :] = off_ref[...]
    part = jnp.zeros((vecs, transfer_ref.shape[2]), jnp.float32)
    for i in range(leaves):
        leaf = vec_ref[:, i * points : (i + 1) * points]
        coeff = dot(leaf, basis_ref[i], nt_dims).astype(jnp.bfloat16)
        part = part + dot(coeff, transfer_ref[i], nn_dims)
        packed = pack(coeff)
        for c in range(copies):
            big_ref[c, i * rows : (i + 1) * rows, :] = packed
    coupling = pack(group_ref[0, 0])
    packed_part = pack(part)
    for c in range(copies):
        big_ref[c, leaves * rows :, :] = coupling
        small_ref[c] = packed_part


def coarse_kernel(small_ref, out_ref):
    total = small_ref[0]
    for i in range(1, small_ref.shape[0]):
        total = total + small_ref[i]
    rounded = total.astype(jnp.bfloat16)
    for i in range(out_ref.shape[0]):
        out_ref[i] = rounded


def spread(ids, axis_pos):
    total = jnp.zeros_like(ids)
    for b in range(id_bits):
        bit = jnp.bitwise_and(jnp.right_shift(ids, 3 * b + axis_pos), 1)
        total = total + jnp.left_shift(bit, b)
    return total


def pieces(x):
    first = x.astype(jnp.bfloat16).astype(jnp.float32)
    second = (x - first).astype(jnp.bfloat16).astype(jnp.float32)
    return first, second, (x - first) - second


def near_kernel(list_ref, count_ref, own_ref, before_ref, after_ref, out_ref, source, target, vecs, wide):
    leaves, vec_count, width = out_ref.shape
    n = leaves * width
    base = list_ref[0, 0]
    rows = lax.broadcasted_iota(jnp.int32, (8, n), 0)
    lanes = lax.broadcasted_iota(jnp.int32, (8, n), 1)
    middle = spread(jnp.full((8, n), base, jnp.int32), rows) + jnp.where(rows == 0, 2, 1)
    vecs[3 * leaves] = jnp.zeros((vec_count, width), jnp.bfloat16)
    wide[...] = jnp.zeros((8, n), jnp.float32)
    for w, ref in enumerate((before_ref, own_ref, after_ref)):
        for i in range(leaves):
            vecs[w * leaves + i] = ref[0:vec_count, i * width : (i + 1) * width]
        wide[0:3, :] = ref[vec_count : vec_count + 3, :].astype(jnp.float32)
        o = wide[...]
        ids = base + (w - 1) * leaves + jnp.right_shift(lanes, 8)
        c = jnp.where(rows < 3, spread(ids, rows) - middle, 0).astype(jnp.float32)
        p = o + c
        norm = jnp.sum(p * p, axis=0, keepdims=True)
        n1, n2, n3 = pieces(norm)
        tail = jnp.where(rows < 6, 1.0, 0.0)
        tail = jnp.where(rows == 0, n1, jnp.where(rows == 1, n2, jnp.where(rows == 2, n3, tail)))
        blocks = [
            jnp.concatenate([o, o], axis=0).astype(jnp.bfloat16),
            jnp.concatenate([c, c], axis=0).astype(jnp.bfloat16),
            jnp.concatenate([tail, jnp.zeros_like(tail)], axis=0).astype(jnp.bfloat16),
        ]
        blank = jnp.zeros((feature_depth - 48, width), jnp.bfloat16)
        for i in range(leaves):
            span = slice(i * width, (i + 1) * width)
            for j, block in enumerate(blocks):
                source[w * leaves + i, 16 * j : 16 * (j + 1), :] = block[:, span]
            source[w * leaves + i, 48:, :] = blank
        if w == 1:
            t1, t2, t3 = pieces(norm + soften)
            tail = jnp.where(rows == 3, t1, jnp.where(rows == 4, t2, jnp.where(rows == 5, t3, 0.0)))
            tail = jnp.where(rows < 3, 1.0, tail)
            blank = jnp.zeros((feature_depth - 40, width), jnp.float32)
            for i in range(leaves):
                span = slice(i * width, (i + 1) * width)
                o_part, c_part = -2.0 * o[:, span], -2.0 * c[:, span]
                full = jnp.concatenate([o_part, c_part, o_part, c_part, tail[:, span], blank], axis=0)
                target[i] = jnp.transpose(full).astype(jnp.bfloat16)

    def one_leaf(t, carry):
        count = count_ref[t]
        points = target[t]

        def step(i, total):
            for g in range(slots_at_once):
                k = i * slots_at_once + g
                place = list_ref[t, k] - base + leaves
                squared = dot(points, source[place], nn_dims)
                tile = lax.rsqrt(squared).astype(jnp.bfloat16)
                total = total + dot(vecs[jnp.where(k < count, place, 3 * leaves)], tile, nt_dims)
            return total

        steps = (count + slots_at_once - 1) // slots_at_once
        total = lax.fori_loop(0, steps, step, jnp.zeros((vec_count, width), jnp.float32))
        out_ref[t] = total * inv_four_pi
        return carry

    lax.fori_loop(0, leaves, one_leaf, 0)


def far_kernel(list_ref, count_ref, big_ref, coupling_ref, out_ref):
    leaves, slots = coupling_ref.shape[:2]
    group_leaves = big_ref.shape[0] * leaves
    vec_count, rank = out_ref.shape[1:]
    rows = vec_count // 2

    def one_leaf(t, carry):
        count = count_ref[t]

        def step(i, total):
            for g in range(4):
                k = i * 4 + g
                j = lax.rem(list_ref[t, k], group_leaves)
                first = pl.multiple_of(lax.rem(j, leaves) * rows, rows)
                block = unpack(big_ref[lax.div(j, leaves), pl.ds(first, rows), :])
                block = jnp.where(k < count, block, jnp.zeros_like(block))
                total = total + dot(block, coupling_ref[t, k], nt_dims)
            return total

        out_ref[t] = lax.fori_loop(0, (count + 3) // 4, step, jnp.zeros((vec_count, rank), jnp.float32))
        return carry

    lax.fori_loop(0, leaves, one_leaf, 0)


def down_kernel(
    list_ref, count_ref, coarse_ref, big_ref, far_ref, near_ref, transfer_ref, basis_ref, out_ref
):
    leaves, vec_count, rank = far_ref.shape
    width = basis_ref.shape[2]
    coupling_row = leaves * (vec_count // 2)
    total = jnp.zeros((vec_count, rank), jnp.float32)
    for k in range(list_ref.shape[1]):
        block = unpack(coarse_ref[list_ref[0, k]])
        block = jnp.where(k < count_ref[0], block, jnp.zeros_like(block))
        total = total + dot(block, unpack(big_ref[k, coupling_row:, :]), nt_dims)
    coarse_out = total.astype(jnp.bfloat16)
    for i in range(leaves):
        local = far_ref[i] + dot(coarse_out, transfer_ref[i], nt_dims)
        result = near_ref[i] + dot(local.astype(jnp.bfloat16), basis_ref[i], nn_dims)
        out_ref[:, i * width : (i + 1) * width] = result.astype(jnp.bfloat16)


def cost(flops, moved, special=0):
    return pl.CostEstimate(flops=flops, bytes_accessed=moved, transcendentals=special)


def body(
    vectors,
    offsets,
    near_list,
    near_count,
    leaf_basis,
    far_list,
    far_count,
    leaf_coupling,
    transfer,
    group_list,
    group_count,
    group_coupling,
):
    members = lax.axis_size("leaf")
    groups = lax.axis_size("grp")
    vec_count, points = vectors.shape
    leaves, rank, width = leaf_basis.shape
    rows = vec_count // 2
    big_rows = leaves * rows + rank // 2
    stacked = vec_count + offsets.shape[0]
    up = [(i, i + 1) for i in range(members - 1)]
    down = [(j, i) for i, j in up]
    halo, big, small = pl.pallas_call(
        upward_kernel,
        out_shape=(
            jax.ShapeDtypeStruct((stacked, points), jnp.bfloat16),
            jax.ShapeDtypeStruct((members, big_rows, 2 * rank), jnp.bfloat16),
            jax.ShapeDtypeStruct((members, rows, 2 * rank), jnp.float32),
        ),
        in_specs=[vmem] * 5,
        out_specs=(vmem, vmem, vmem),
        compiler_params=params,
        cost_estimate=cost(40_000_000, 3_000_000),
        name="upward",
    )(vectors, offsets, leaf_basis, transfer, group_coupling)
    small_all = lax.all_to_all(small, "leaf", 0, 0, tiled=True)
    before = lax.ppermute(halo, "leaf", up)
    after = lax.ppermute(halo, "leaf", down)
    big_all = lax.all_to_all(big, "leaf", 0, 0, tiled=True)
    coarse = pl.pallas_call(
        coarse_kernel,
        out_shape=jax.ShapeDtypeStruct((groups, rows, 2 * rank), jnp.bfloat16),
        in_specs=[vmem],
        out_specs=vmem,
        compiler_params=params,
        cost_estimate=cost(40_000, 300_000),
        name="coarse",
    )(small_all)
    coarse_all = lax.all_to_all(coarse, "grp", 0, 0, tiled=True)
    near = pl.pallas_call(
        near_kernel,
        out_shape=jax.ShapeDtypeStruct((leaves, vec_count, width), jnp.float32),
        in_specs=[smem, smem, vmem, vmem, vmem],
        out_specs=vmem,
        scratch_shapes=[
            pltpu.VMEM((3 * leaves, feature_depth, width), jnp.bfloat16),
            pltpu.VMEM((leaves, width, feature_depth), jnp.bfloat16),
            pltpu.VMEM((3 * leaves + 1, vec_count, width), jnp.bfloat16),
            pltpu.VMEM((8, points), jnp.float32),
        ],
        compiler_params=params,
        cost_estimate=cost(16_000_000_000, 3_000_000, 15_000_000),
        name="near",
    )(near_list, near_count, halo, before, after)
    far = pl.pallas_call(
        far_kernel,
        out_shape=jax.ShapeDtypeStruct((leaves, vec_count, rank), jnp.float32),
        in_specs=[smem, smem, vmem, vmem],
        out_specs=vmem,
        compiler_params=params,
        cost_estimate=cost(1_000_000_000, 5_000_000),
        name="far",
    )(far_list, far_count, big_all, leaf_coupling)
    return pl.pallas_call(
        down_kernel,
        out_shape=jax.ShapeDtypeStruct((vec_count, points), jnp.bfloat16),
        in_specs=[smem, smem] + [vmem] * 6,
        out_specs=vmem,
        compiler_params=params,
        cost_estimate=cost(100_000_000, 3_000_000),
        name="downward",
    )(group_list, group_count, coarse_all, big_all, far, near, transfer, leaf_basis)


def solution(mesh):
    both = ("grp", "leaf")
    placed = (
        P(None, both),
        P(None, both),
        P(both, None),
        P(both),
        P(both, None, None),
        P(both, None),
        P(both),
        P(both, None, None, None),
        P(both, None, None),
        P("grp", None),
        P("grp"),
        P("grp", "leaf", None, None),
    )
    return jax.shard_map(body, mesh=mesh, in_specs=placed, out_specs=P(None, both), check_vma=False)
```

```python
import jax
import jax.numpy as jnp
from jax import lax
from jax.experimental import pallas as pl
from jax.experimental.pallas import tpu as pltpu
from jax.sharding import Mesh
from jax.sharding import PartitionSpec as P

inv_four_pi = 0.07957747154594767
soften = 0.01
sharpness = inv_four_pi**-2
feature_depth = 64
near_at_once = 4
far_at_once = 8
id_bits = 5
deep = 4
vmem_bytes = 50 << 20
whole_bytes = 63 << 20

nt_dims = (((1,), (1,)), ((), ()))
nn_dims = (((1,), (0,)), ((), ()))
smem = pl.BlockSpec(memory_space=pltpu.SMEM)
vmem = pl.BlockSpec(memory_space=pltpu.VMEM)
hbm = pl.BlockSpec(memory_space=pltpu.HBM)
params = pltpu.CompilerParams(vmem_limit_bytes=vmem_bytes)
whole = pltpu.CompilerParams(vmem_limit_bytes=whole_bytes)
anywhere = pl.BlockSpec(memory_space=pl.ANY)


def dot(left, right, dims):
    return lax.dot_general(left, right, dims, preferred_element_type=jnp.float32)


def pack(block):
    half = block.shape[0] // 2
    return jnp.concatenate([block[:half], block[half:]], axis=1)


def unpack(block):
    half = block.shape[1] // 2
    return jnp.concatenate([block[:, :half], block[:, half:]], axis=0)


def upward_kernel(
    vec_hbm, off_hbm, basis_hbm, transfer_hbm, group_hbm, halo_ref, big_ref, *scratch
):
    vec_ref, off_ref, basis_ref, transfer_ref, group_ref, sems = scratch
    sources = (vec_hbm, off_hbm, basis_hbm, transfer_hbm, group_hbm)
    copies_in = [
        pltpu.make_async_copy(src, dst, sems.at[i])
        for i, (src, dst) in enumerate(zip(sources, scratch[:5]))
    ]
    for copy in copies_in:
        copy.start()
    vecs, width = vec_ref.shape
    leaves = basis_ref.shape[0]
    points = width // leaves
    copies = big_ref.shape[0]
    rows = vecs // 2
    for copy in copies_in:
        copy.wait()
    halo_ref[0:vecs, :] = vec_ref[...]
    halo_ref[vecs : vecs + off_ref.shape[0], :] = off_ref[...]
    part = jnp.zeros((vecs, transfer_ref.shape[2]), jnp.float32)
    for i in range(leaves):
        leaf = vec_ref[:, i * points : (i + 1) * points]
        coeff = dot(leaf, basis_ref[i], nt_dims).astype(jnp.bfloat16)
        part = part + dot(coeff, transfer_ref[i], nn_dims)
        packed = pack(coeff)
        for c in range(copies):
            big_ref[c, i * rows : (i + 1) * rows, :] = packed
    coupling = pack(group_ref[0, 0])
    packed_part = pack(part)
    high = packed_part.astype(jnp.bfloat16)
    low = (packed_part - high.astype(jnp.float32)).astype(jnp.bfloat16)
    first = leaves * rows + coupling.shape[0]
    for c in range(copies):
        big_ref[c, leaves * rows : first, :] = coupling
        big_ref[c, first : first + rows, :] = high
        big_ref[c, first + rows :, :] = low


def regroup_kernel(big_ref, out_ref):
    deep, big_rows = big_ref.shape[:2]
    keep = (out_ref.shape[1] - big_rows) // (deep - 1)
    rows = (big_rows - keep) // 2
    total = jnp.zeros((rows, big_ref.shape[2]), jnp.float32)
    for i in range(deep):
        high = big_ref[i, keep : keep + rows, :].astype(jnp.float32)
        total = total + (high + big_ref[i, keep + rows :, :].astype(jnp.float32))
    high = total.astype(jnp.bfloat16)
    low = (total - high.astype(jnp.float32)).astype(jnp.bfloat16)
    for c in range(out_ref.shape[0]):
        for i in range(deep):
            out_ref[c, i * keep : (i + 1) * keep, :] = big_ref[i, :keep, :]
        out_ref[c, deep * keep : deep * keep + rows, :] = high
        out_ref[c, deep * keep + rows :, :] = low


def coarse_kernel(big_ref, near_ref, out_ref):
    members, big_rows = big_ref.shape[:2]
    rows = out_ref.shape[1]
    total = jnp.zeros(out_ref.shape[1:], jnp.float32)
    for i in range(members):
        high = big_ref[i, big_rows - 2 * rows : big_rows - rows, :].astype(jnp.float32)
        total = total + (high + big_ref[i, big_rows - rows :, :].astype(jnp.float32))
    rounded = total.astype(jnp.bfloat16)
    for i in range(out_ref.shape[0]):
        out_ref[i] = rounded


def spread(ids, axis_pos):
    total = jnp.zeros_like(ids)
    for b in range(id_bits):
        bit = jnp.bitwise_and(jnp.right_shift(ids, 3 * b + axis_pos), 1)
        total = total + jnp.left_shift(bit, b)
    return total


def pieces(x):
    first = x.astype(jnp.bfloat16).astype(jnp.float32)
    second = (x - first).astype(jnp.bfloat16).astype(jnp.float32)
    return first, second, (x - first) - second


def list_pairs(count_ref, leaves, chunk, put, pad):
    def one_leaf(t, place):
        return lax.fori_loop(0, count_ref[t], lambda k, q: put(t, k, q), place)

    total = lax.fori_loop(0, leaves, one_leaf, 0)
    chunks = (total + chunk - 1) // chunk

    def fill(q, carry):
        pad(q)
        return carry

    lax.fori_loop(total, chunks * chunk + chunk, fill, 0)
    return chunks


def near_kernel(
    list_ref, count_ref, own_ref, before_ref, after_ref, first_ref, out_ref, *scratch
):
    source, target, vecs, wide, to_leaf, from_leaf, tiles_a, tiles_b = scratch
    leaves = out_ref.shape[0] - 1
    vec_count, width = out_ref.shape[1:]
    n = leaves * width
    base = list_ref[0, 0]
    rows = lax.broadcasted_iota(jnp.int32, (8, n), 0)
    lanes = lax.broadcasted_iota(jnp.int32, (8, n), 1)
    middle = spread(jnp.full((8, n), base, jnp.int32), rows) + jnp.where(rows == 0, 2, 1)
    wide[...] = jnp.zeros((8, n), jnp.float32)
    blank = jnp.zeros((128 - 56, width), jnp.float32)
    for w, ref in enumerate((before_ref, own_ref, after_ref)):
        for i in range(leaves):
            vecs[w * leaves + i] = ref[0:vec_count, i * width : (i + 1) * width]
        wide[0:3, :] = ref[vec_count : vec_count + 3, :].astype(jnp.float32)
        o = wide[...]
        ids = base + (w - 1) * leaves + jnp.right_shift(lanes, 8)
        c = jnp.where(rows < 3, spread(ids, rows) - middle, 0).astype(jnp.float32)
        p = o + c
        norm = jnp.sum(p * p, axis=0, keepdims=True)
        n1, n2, n3 = pieces(norm * sharpness)
        tail = jnp.where(rows < 6, 1.0, 0.0)
        tail = jnp.where(rows == 0, n1, jnp.where(rows == 1, n2, jnp.where(rows == 2, n3, tail)))
        for i in range(leaves):
            span = slice(i * width, (i + 1) * width)
            o_part, c_part = o[:, span], c[:, span]
            full = jnp.concatenate([o_part] * 3 + [c_part] * 3 + [tail[:, span], blank], axis=0)
            source[w * leaves + i] = jnp.transpose(full).astype(jnp.bfloat16)
        if w == 1:
            t1, t2, t3 = pieces((norm + soften) * sharpness)
            p1, p2, p3 = pieces(p * (-2.0 * sharpness))
            tail = jnp.where(rows == 3, t1, jnp.where(rows == 4, t2, jnp.where(rows == 5, t3, 0.0)))
            tail = jnp.where(rows < 3, 1.0, tail)
            halves = [(p1, p2), (p3, p1), (p2, p3), (tail, jnp.zeros_like(tail))]
            for j, pair in enumerate(halves):
                block = jnp.concatenate(pair, axis=0).astype(jnp.bfloat16)
                for i in range(leaves):
                    target[i, 16 * j : 16 * (j + 1), :] = block[:, i * width : (i + 1) * width]

    def put(t, k, q):
        to_leaf[q] = t
        from_leaf[q] = list_ref[t, k] - base + leaves
        return q + 1

    def pad(q):
        to_leaf[q] = leaves
        from_leaf[q] = 0

    pairs = list_pairs(count_ref, leaves, 2 * near_at_once, put, pad)
    out_ref[...] = jnp.zeros_like(out_ref)

    def make_tiles(first, tiles):
        for g in range(near_at_once):
            t = jnp.minimum(to_leaf[first + g], leaves - 1)
            points = source[from_leaf[first + g]][:, :feature_depth]
            tiles[g] = lax.rsqrt(dot(points, target[t], nn_dims)).astype(jnp.bfloat16)

    def use_tiles(first, tiles):
        for g in range(near_at_once):
            out_ref[to_leaf[first + g]] += dot(vecs[from_leaf[first + g]], tiles[g], nn_dims)

    make_tiles(0, tiles_a)

    def step(i, carry):
        first = 2 * near_at_once * i
        make_tiles(first + near_at_once, tiles_b)
        use_tiles(first, tiles_a)
        make_tiles(first + 2 * near_at_once, tiles_a)
        use_tiles(first + near_at_once, tiles_b)
        return carry

    lax.fori_loop(0, pairs, step, 0)


def far_kernel(list_ref, count_ref, big_ref, coupling_ref, out_ref, to_leaf, slot, from_leaf):
    leaves, slots = coupling_ref.shape[:2]
    across = big_ref.shape[0]
    rows = out_ref.shape[1] // 2
    keep = leaves * rows + coupling_ref.shape[2] // 2
    group_leaves = across * deep * leaves

    def put(t, k, q):
        to_leaf[q] = t
        slot[q] = k
        from_leaf[q] = lax.rem(list_ref[t, k], group_leaves)
        return q + 1

    def pad(q):
        to_leaf[q] = leaves
        slot[q] = 0
        from_leaf[q] = 0

    chunks = list_pairs(count_ref, leaves, far_at_once, put, pad)
    out_ref[...] = jnp.zeros_like(out_ref)

    def step(i, carry):
        terms = []
        for g in range(far_at_once):
            q = i * far_at_once + g
            j = from_leaf[q]
            holder = lax.div(j, leaves)
            first = lax.div(holder, across) * keep + lax.rem(j, leaves) * rows
            first = pl.multiple_of(first, rows)
            block = unpack(big_ref[lax.rem(holder, across), pl.ds(first, rows), :])
            coupling = coupling_ref[jnp.minimum(to_leaf[q], leaves - 1), slot[q]]
            terms.append(dot(block, coupling, nt_dims))
        for g, term in enumerate(terms):
            out_ref[to_leaf[i * far_at_once + g]] += term
        return carry

    lax.fori_loop(0, chunks, step, 0)


def down_kernel(
    list_ref, count_ref, coarse_ref, big_ref, far_ref, near_ref, transfer_ref, basis_ref, out_ref
):
    leaves, rank, width = basis_ref.shape
    vec_count = out_ref.shape[0]
    across = big_ref.shape[0]
    keep = leaves * (vec_count // 2) + rank // 2
    total = jnp.zeros((vec_count, rank), jnp.float32)
    for k in range(list_ref.shape[1]):
        block = unpack(coarse_ref[list_ref[0, k]])
        block = jnp.where(k < count_ref[0], block, jnp.zeros_like(block))
        last = (k // across + 1) * keep
        coupling = unpack(big_ref[k % across, last - rank // 2 : last, :])
        total = total + dot(block, coupling, nt_dims)
    coarse_out = total.astype(jnp.bfloat16)
    for i in range(leaves):
        local = far_ref[i] + dot(coarse_out, transfer_ref[i], nt_dims)
        result = near_ref[i] + dot(local.astype(jnp.bfloat16), basis_ref[i], nn_dims)
        out_ref[:, i * width : (i + 1) * width] = result.astype(jnp.bfloat16)


def cost(flops, moved, special=0):
    return pl.CostEstimate(flops=flops, bytes_accessed=moved, transcendentals=special)


def body(
    vectors,
    offsets,
    near_list,
    near_count,
    leaf_basis,
    far_list,
    far_count,
    leaf_coupling,
    transfer,
    group_list,
    group_count,
    group_coupling,
):
    across = lax.axis_size("across")
    members = lax.axis_size("deep") * across
    groups = lax.axis_size("grp")
    vec_count, points = vectors.shape
    leaves, rank, width = leaf_basis.shape
    rows = vec_count // 2
    keep = leaves * rows + rank // 2
    stacked = vec_count + offsets.shape[0]
    up = [(i, i + 1) for i in range(members - 1)]
    down = [(j, i) for i, j in up]
    inputs = (vectors, offsets, leaf_basis, transfer, group_coupling)
    halo, big = pl.pallas_call(
        upward_kernel,
        out_shape=(
            jax.ShapeDtypeStruct((stacked, points), jnp.bfloat16),
            jax.ShapeDtypeStruct((deep, keep + 2 * rows, 2 * rank), jnp.bfloat16),
        ),
        in_specs=[hbm] * 5,
        out_specs=(vmem, vmem),
        scratch_shapes=[pltpu.VMEM(x.shape, x.dtype) for x in inputs]
        + [pltpu.SemaphoreType.DMA((len(inputs),))],
        compiler_params=whole,
        cost_estimate=cost(40_000_000, 3_000_000),
        name="upward",
    )(*inputs)
    deep_all = lax.all_to_all(big, "deep", 0, 0, tiled=True)
    before = lax.ppermute(halo, ("deep", "across"), up)
    after = lax.ppermute(halo, ("deep", "across"), down)
    wide = pl.pallas_call(
        regroup_kernel,
        out_shape=jax.ShapeDtypeStruct((across, deep * keep + 2 * rows, 2 * rank), jnp.bfloat16),
        in_specs=[vmem],
        out_specs=vmem,
        compiler_params=params,
        cost_estimate=cost(40_000, 2_000_000),
        name="regroup",
    )(deep_all)
    big_all = lax.all_to_all(wide, "across", 0, 0, tiled=True)
    near_pairs = near_list.size + 4 * near_at_once
    far_pairs = far_list.size + 2 * far_at_once
    near = pl.pallas_call(
        near_kernel,
        out_shape=jax.ShapeDtypeStruct((leaves + 1, vec_count, width), jnp.float32),
        in_specs=[smem, smem, vmem, vmem, vmem, anywhere],
        out_specs=vmem,
        scratch_shapes=[
            pltpu.VMEM((3 * leaves, width, 128), jnp.bfloat16),
            pltpu.VMEM((leaves, feature_depth, width), jnp.bfloat16),
            pltpu.VMEM((3 * leaves, vec_count, width), jnp.bfloat16),
            pltpu.VMEM((8, points), jnp.float32),
            pltpu.SMEM((near_pairs,), jnp.int32),
            pltpu.SMEM((near_pairs,), jnp.int32),
            pltpu.VMEM((near_at_once, width, width), jnp.bfloat16),
            pltpu.VMEM((near_at_once, width, width), jnp.bfloat16),
        ],
        compiler_params=params,
        cost_estimate=cost(16_000_000_000, 3_000_000, 15_000_000),
        name="near",
    )(near_list, near_count, halo, before, after, wide)
    coarse = pl.pallas_call(
        coarse_kernel,
        out_shape=jax.ShapeDtypeStruct((groups, rows, 2 * rank), jnp.bfloat16),
        in_specs=[vmem, anywhere],
        out_specs=vmem,
        compiler_params=params,
        cost_estimate=cost(40_000, 300_000),
        name="coarse",
    )(big_all, near)
    coarse_all = lax.all_to_all(coarse, "grp", 0, 0, tiled=True)
    far = pl.pallas_call(
        far_kernel,
        out_shape=jax.ShapeDtypeStruct((leaves + 1, vec_count, rank), jnp.float32),
        in_specs=[smem, smem, vmem, vmem],
        out_specs=vmem,
        scratch_shapes=[pltpu.SMEM((far_pairs,), jnp.int32) for _ in range(3)],
        compiler_params=params,
        cost_estimate=cost(1_000_000_000, 5_000_000),
        name="far",
    )(far_list, far_count, big_all, leaf_coupling)
    return pl.pallas_call(
        down_kernel,
        out_shape=jax.ShapeDtypeStruct((vec_count, points), jnp.bfloat16),
        in_specs=[smem, smem] + [vmem] * 6,
        out_specs=vmem,
        compiler_params=params,
        cost_estimate=cost(100_000_000, 3_000_000),
        name="downward",
    )(group_list, group_count, coarse_all, big_all, far, near, transfer, leaf_basis)


def solution(mesh):
    groups, members = mesh.devices.shape
    split = Mesh(mesh.devices.reshape(groups, deep, members // deep), ("grp", "deep", "across"))
    leaf = ("deep", "across")
    both = ("grp",) + leaf
    placed = (
        P(None, both),
        P(None, both),
        P(both, None),
        P(both),
        P(both, None, None),
        P(both, None),
        P(both),
        P(both, None, None, None),
        P(both, None, None),
        P("grp", None),
        P("grp"),
        P("grp", leaf, None, None),
    )
    return jax.shard_map(body, mesh=split, in_specs=placed, out_specs=P(None, both), check_vma=False)
```

```python
import jax
import jax.numpy as jnp
from jax import lax
from jax.experimental import pallas as pl
from jax.experimental.pallas import tpu as pltpu
from jax.sharding import Mesh
from jax.sharding import PartitionSpec as P

inv_four_pi = 0.07957747154594767
soften = 0.01
sharpness = inv_four_pi**-2
feature_depth = 64
near_at_once = 6
far_at_once = 16
far_shift = 7
id_bits = 5
deep = 4
vmem_bytes = 20 << 20
whole_bytes = 63 << 20

nt_dims = (((1,), (1,)), ((), ()))
nn_dims = (((1,), (0,)), ((), ()))
smem = pl.BlockSpec(memory_space=pltpu.SMEM)
vmem = pl.BlockSpec(memory_space=pltpu.VMEM)
hbm = pl.BlockSpec(memory_space=pltpu.HBM)
params = pltpu.CompilerParams(vmem_limit_bytes=vmem_bytes)
whole = pltpu.CompilerParams(vmem_limit_bytes=whole_bytes)
anywhere = pl.BlockSpec(memory_space=pl.ANY)


def dot(left, right, dims):
    return lax.dot_general(left, right, dims, preferred_element_type=jnp.float32)


def pack(block):
    half = block.shape[0] // 2
    return jnp.concatenate([block[:half], block[half:]], axis=1)


def unpack(block):
    half = block.shape[1] // 2
    return jnp.concatenate([block[:, :half], block[:, half:]], axis=0)


def upward_kernel(
    vec_hbm, off_hbm, basis_hbm, transfer_hbm, group_hbm, halo_ref, big_ref, *scratch
):
    vec_ref, off_ref, basis_ref, transfer_ref, group_ref, sems = scratch
    sources = (vec_hbm, off_hbm, basis_hbm, transfer_hbm, group_hbm)
    copies_in = [
        pltpu.make_async_copy(src, dst, sems.at[i])
        for i, (src, dst) in enumerate(zip(sources, scratch[:5]))
    ]
    for copy in copies_in:
        copy.start()
    vecs, width = vec_ref.shape
    leaves = basis_ref.shape[0]
    points = width // leaves
    copies = big_ref.shape[0]
    rows = vecs // 2
    copies_in[0].wait()
    copies_in[1].wait()
    halo_ref[0:vecs, :] = vec_ref[...]
    halo_ref[vecs : vecs + off_ref.shape[0], :] = off_ref[...]
    for copy in copies_in[2:]:
        copy.wait()
    part = jnp.zeros((vecs, transfer_ref.shape[2]), jnp.float32)
    for i in range(leaves):
        leaf = vec_ref[:, i * points : (i + 1) * points]
        coeff = dot(leaf, basis_ref[i], nt_dims).astype(jnp.bfloat16)
        part = part + dot(coeff, transfer_ref[i], nn_dims)
        packed = pack(coeff)
        for c in range(copies):
            big_ref[c, i * rows : (i + 1) * rows, :] = packed
    coupling = pack(group_ref[0, 0])
    packed_part = pack(part)
    high = packed_part.astype(jnp.bfloat16)
    low = (packed_part - high.astype(jnp.float32)).astype(jnp.bfloat16)
    first = leaves * rows + coupling.shape[0]
    for c in range(copies):
        big_ref[c, leaves * rows : first, :] = coupling
        big_ref[c, first : first + rows, :] = high
        big_ref[c, first + rows :, :] = low


def regroup_kernel(big_ref, out_ref):
    deep, big_rows = big_ref.shape[:2]
    keep = (out_ref.shape[1] - big_rows) // (deep - 1)
    rows = (big_rows - keep) // 2
    total = jnp.zeros((rows, big_ref.shape[2]), jnp.float32)
    for i in range(deep):
        high = big_ref[i, keep : keep + rows, :].astype(jnp.float32)
        total = total + (high + big_ref[i, keep + rows :, :].astype(jnp.float32))
    high = total.astype(jnp.bfloat16)
    low = (total - high.astype(jnp.float32)).astype(jnp.bfloat16)
    for c in range(out_ref.shape[0]):
        for i in range(deep):
            out_ref[c, i * keep : (i + 1) * keep, :] = big_ref[i, :keep, :]
        out_ref[c, deep * keep : deep * keep + rows, :] = high
        out_ref[c, deep * keep + rows :, :] = low


def coarse_kernel(big_ref, near_ref, out_ref):
    members, big_rows = big_ref.shape[:2]
    rows = out_ref.shape[0]
    total = jnp.zeros(out_ref.shape, jnp.float32)
    for i in range(members):
        high = big_ref[i, big_rows - 2 * rows : big_rows - rows, :].astype(jnp.float32)
        total = total + (high + big_ref[i, big_rows - rows :, :].astype(jnp.float32))
    out_ref[...] = total.astype(jnp.bfloat16)


def both_kernel(own_ref, other_ref, far_ref, out_ref):
    rows = own_ref.shape[0]
    half = lax.axis_index("half")
    for i in range(out_ref.shape[0]):
        out_ref[i, pl.ds(pl.multiple_of(half * rows, rows), rows), :] = own_ref[...]
        out_ref[i, pl.ds(pl.multiple_of((1 - half) * rows, rows), rows), :] = other_ref[...]


def spread(ids, axis_pos):
    total = jnp.zeros_like(ids)
    for b in range(id_bits):
        bit = jnp.bitwise_and(jnp.right_shift(ids, 3 * b + axis_pos), 1)
        total = total + jnp.left_shift(bit, b)
    return total


def pieces(x):
    first = x.astype(jnp.bfloat16).astype(jnp.float32)
    second = (x - first).astype(jnp.bfloat16).astype(jnp.float32)
    return first, second, (x - first) - second


def near_kernel(
    list_ref, count_ref, own_ref, before_ref, after_ref, first_ref, out_ref, *scratch
):
    source, target, vecs, wide, to_leaf, from_leaf, tiles_a, tiles_b = scratch
    leaves = out_ref.shape[0] - 1
    vec_count, width = out_ref.shape[1:]
    slots = list_ref.shape[1]
    n = leaves * width
    base = list_ref[0, 0]
    rows = lax.broadcasted_iota(jnp.int32, (8, n), 0)
    lanes = lax.broadcasted_iota(jnp.int32, (8, n), 1)
    middle = spread(jnp.full((8, n), base, jnp.int32), rows) + jnp.where(rows == 0, 2, 1)
    wide[...] = jnp.zeros((8, n), jnp.float32)
    blank = jnp.zeros((128 - 56, width), jnp.float32)
    for w, ref in enumerate((before_ref, own_ref, after_ref)):
        for i in range(leaves):
            vecs[w * leaves + i] = ref[0:vec_count, i * width : (i + 1) * width]
        wide[0:3, :] = ref[vec_count : vec_count + 3, :].astype(jnp.float32)
        o = wide[...]
        ids = base + (w - 1) * leaves + jnp.right_shift(lanes, 8)
        c = jnp.where(rows < 3, spread(ids, rows) - middle, 0).astype(jnp.float32)
        p = o + c
        norm = jnp.sum(p * p, axis=0, keepdims=True)
        n1, n2, n3 = pieces(norm * sharpness)
        tail = jnp.where(rows < 6, 1.0, 0.0)
        tail = jnp.where(rows == 0, n1, jnp.where(rows == 1, n2, jnp.where(rows == 2, n3, tail)))
        for i in range(leaves):
            span = slice(i * width, (i + 1) * width)
            o_part, c_part = o[:, span], c[:, span]
            full = jnp.concatenate([o_part] * 3 + [c_part] * 3 + [tail[:, span], blank], axis=0)
            source[w * leaves + i] = jnp.transpose(full).astype(jnp.bfloat16)
        if w == 1:
            t1, t2, t3 = pieces((norm + soften) * sharpness)
            p1, p2, p3 = pieces(p * (-2.0 * sharpness))
            tail = jnp.where(rows == 3, t1, jnp.where(rows == 4, t2, jnp.where(rows == 5, t3, 0.0)))
            tail = jnp.where(rows < 3, 1.0, tail)
            halves = [(p1, p2), (p3, p1), (p2, p3), (tail, jnp.zeros_like(tail))]
            for j, pair in enumerate(halves):
                block = jnp.concatenate(pair, axis=0).astype(jnp.bfloat16)
                for i in range(leaves):
                    target[i, 16 * j : 16 * (j + 1), :] = block[:, i * width : (i + 1) * width]

    def one_leaf(t, q):
        count = count_ref[t]
        for k in range(slots):
            to_leaf[q] = t
            from_leaf[q] = list_ref[t, k] - base + leaves
            q = q + jnp.where(k < count, 1, 0)
        return q

    total = lax.fori_loop(0, leaves, one_leaf, 0)
    for g in range(3 * near_at_once):
        to_leaf[total + g] = leaves
        from_leaf[total + g] = 0
    chunk = 2 * near_at_once
    chunks = lax.div(total + (chunk - 1), chunk)
    out_ref[...] = jnp.zeros_like(out_ref)

    def make_tiles(first, tiles):
        for g in range(near_at_once):
            t = jnp.minimum(to_leaf[first + g], leaves - 1)
            points = source[from_leaf[first + g]][:, :feature_depth]
            tiles[g] = lax.rsqrt(dot(points, target[t], nn_dims)).astype(jnp.bfloat16)

    def use_tiles(first, tiles):
        for g in range(near_at_once):
            out_ref[to_leaf[first + g]] += dot(vecs[from_leaf[first + g]], tiles[g], nn_dims)

    make_tiles(0, tiles_a)

    def step(i, carry):
        first = 2 * near_at_once * i
        make_tiles(first + near_at_once, tiles_b)
        use_tiles(first, tiles_a)
        make_tiles(first + 2 * near_at_once, tiles_a)
        use_tiles(first + near_at_once, tiles_b)
        return carry

    lax.fori_loop(0, chunks, step, 0)


def far_kernel(list_ref, count_ref, big_ref, coupling_ref, first_ref, out_ref, *scratch):
    to_leaf, pair, from_leaf = scratch
    leaves, slots = coupling_ref.shape[:2]
    across = big_ref.shape[0]
    rows = out_ref.shape[1] // 2
    keep = leaves * rows + coupling_ref.shape[2] // 2
    leaf_mask, across_mask = leaves - 1, across - 1
    leaf_shift, across_shift = leaves.bit_length() - 1, across.bit_length() - 1
    slot_shift = slots.bit_length() - 1

    def one_leaf(t, q):
        count = count_ref[t]
        for k in range(slots):
            j = jnp.bitwise_and(list_ref[t, k], across * deep * leaves - 1)
            holder = jnp.right_shift(j, leaf_shift)
            to_leaf[q] = t
            pair[q] = t * slots + k
            place = jnp.right_shift(holder, across_shift) * (keep // rows)
            place = place + jnp.bitwise_and(j, leaf_mask)
            from_leaf[q] = jnp.left_shift(jnp.bitwise_and(holder, across_mask), far_shift) + place
            q = q + jnp.where(k < count, 1, 0)
        return q

    total = lax.fori_loop(0, leaves, one_leaf, 0)
    for g in range(far_at_once):
        to_leaf[total + g] = leaves
        pair[total + g] = 0
        from_leaf[total + g] = 0
    out_ref[...] = jnp.zeros_like(out_ref)

    def step(i, carry):
        terms = []
        for g in range(far_at_once):
            q = i * far_at_once + g
            place = from_leaf[q]
            first = jnp.bitwise_and(place, (1 << far_shift) - 1) * rows
            first = pl.multiple_of(first, rows)
            block = unpack(big_ref[jnp.right_shift(place, far_shift), pl.ds(first, rows), :])
            t, k = jnp.right_shift(pair[q], slot_shift), jnp.bitwise_and(pair[q], slots - 1)
            terms.append(dot(block, coupling_ref[t, k], nt_dims))
        for g, term in enumerate(terms):
            out_ref[to_leaf[i * far_at_once + g]] += term
        return carry

    lax.fori_loop(0, lax.div(total + far_at_once - 1, far_at_once), step, 0)


def down_kernel(
    list_ref, count_ref, coarse_ref, big_ref, far_ref, near_ref, transfer_ref, basis_ref, out_ref
):
    leaves, rank, width = basis_ref.shape
    vec_count = out_ref.shape[0]
    across = big_ref.shape[0]
    rows = vec_count // 2
    keep = leaves * rows + rank // 2
    terms = []
    for k in range(list_ref.shape[1]):
        g = list_ref[0, k]
        peer = jnp.bitwise_and(g, 1) + jnp.left_shift(jnp.right_shift(g, 2), 1)
        first = pl.multiple_of(jnp.bitwise_and(jnp.right_shift(g, 1), 1) * rows, rows)
        block = unpack(coarse_ref[peer, pl.ds(first, rows), :])
        block = jnp.where(k < count_ref[0], block, jnp.zeros_like(block))
        last = (k // across + 1) * keep
        coupling = unpack(big_ref[k % across, last - rank // 2 : last, :])
        terms.append(dot(block, coupling, nt_dims))
    while len(terms) > 1:
        terms = [a + b for a, b in zip(terms[::2], terms[1::2])]
    coarse_out = terms[0].astype(jnp.bfloat16)
    for i in range(leaves):
        local = far_ref[i] + dot(coarse_out, transfer_ref[i], nt_dims)
        result = near_ref[i] + dot(local.astype(jnp.bfloat16), basis_ref[i], nn_dims)
        out_ref[:, i * width : (i + 1) * width] = result.astype(jnp.bfloat16)


def cost(flops, moved, special=0):
    return pl.CostEstimate(flops=flops, bytes_accessed=moved, transcendentals=special)


def body(
    vectors,
    offsets,
    near_list,
    near_count,
    leaf_basis,
    far_list,
    far_count,
    leaf_coupling,
    transfer,
    group_list,
    group_count,
    group_coupling,
):
    across = lax.axis_size("across")
    members = lax.axis_size("deep") * across
    vec_count, points = vectors.shape
    leaves, rank, width = leaf_basis.shape
    rows = vec_count // 2
    keep = leaves * rows + rank // 2
    stacked = vec_count + offsets.shape[0]
    up = [(i, i + 1) for i in range(members - 1)]
    down = [(j, i) for i, j in up]
    inputs = (vectors, offsets, leaf_basis, transfer, group_coupling)
    halo, big = pl.pallas_call(
        upward_kernel,
        out_shape=(
            jax.ShapeDtypeStruct((stacked, points), jnp.bfloat16),
            jax.ShapeDtypeStruct((deep, keep + 2 * rows, 2 * rank), jnp.bfloat16),
        ),
        in_specs=[hbm] * 5,
        out_specs=(vmem, vmem),
        scratch_shapes=[pltpu.VMEM(x.shape, x.dtype) for x in inputs]
        + [pltpu.SemaphoreType.DMA((len(inputs),))],
        compiler_params=whole,
        cost_estimate=cost(40_000_000, 3_000_000),
        name="upward",
    )(*inputs)
    deep_all = lax.all_to_all(big, "deep", 0, 0, tiled=True)
    before = lax.ppermute(halo, ("deep", "across"), up)
    after = lax.ppermute(halo, ("deep", "across"), down)
    wide = pl.pallas_call(
        regroup_kernel,
        out_shape=jax.ShapeDtypeStruct((across, deep * keep + 2 * rows, 2 * rank), jnp.bfloat16),
        in_specs=[vmem],
        out_specs=vmem,
        compiler_params=params,
        cost_estimate=cost(40_000, 2_000_000),
        name="regroup",
    )(deep_all)
    big_all = lax.all_to_all(wide, "across", 0, 0, tiled=True)
    near_pairs = near_list.size + 4 * near_at_once
    far_pairs = far_list.size + 2 * far_at_once
    near = pl.pallas_call(
        near_kernel,
        out_shape=jax.ShapeDtypeStruct((leaves + 1, vec_count, width), jnp.float32),
        in_specs=[smem, smem, vmem, vmem, vmem, anywhere],
        out_specs=vmem,
        scratch_shapes=[
            pltpu.VMEM((3 * leaves, width, 128), jnp.bfloat16),
            pltpu.VMEM((leaves, feature_depth, width), jnp.bfloat16),
            pltpu.VMEM((3 * leaves, vec_count, width), jnp.bfloat16),
            pltpu.VMEM((8, points), jnp.float32),
            pltpu.SMEM((near_pairs,), jnp.int32),
            pltpu.SMEM((near_pairs,), jnp.int32),
            pltpu.VMEM((near_at_once, width, width), jnp.bfloat16),
            pltpu.VMEM((near_at_once, width, width), jnp.bfloat16),
        ],
        compiler_params=params,
        cost_estimate=cost(16_000_000_000, 3_000_000, 15_000_000),
        name="near",
    )(near_list, near_count, halo, before, after, wide)
    coarse = pl.pallas_call(
        coarse_kernel,
        out_shape=jax.ShapeDtypeStruct((rows, 2 * rank), jnp.bfloat16),
        in_specs=[vmem, anywhere],
        out_specs=vmem,
        compiler_params=params,
        cost_estimate=cost(40_000, 300_000),
        name="coarse",
    )(big_all, near)
    other = lax.ppermute(coarse, "half", [(0, 1), (1, 0)])
    far = pl.pallas_call(
        far_kernel,
        out_shape=jax.ShapeDtypeStruct((leaves + 1, vec_count, rank), jnp.float32),
        in_specs=[smem, smem, vmem, vmem, anywhere],
        out_specs=vmem,
        scratch_shapes=[pltpu.SMEM((far_pairs,), jnp.int32) for _ in range(3)],
        compiler_params=params,
        cost_estimate=cost(1_000_000_000, 5_000_000),
        name="far",
    )(far_list, far_count, big_all, leaf_coupling, coarse)
    peers = lax.axis_size("row") * lax.axis_size("core")
    both = pl.pallas_call(
        both_kernel,
        out_shape=jax.ShapeDtypeStruct((peers, 2 * rows, 2 * rank), jnp.bfloat16),
        in_specs=[vmem, vmem, anywhere],
        out_specs=vmem,
        compiler_params=params,
        cost_estimate=cost(40_000, 300_000),
        name="both",
    )(coarse, other, far)
    coarse_all = lax.all_to_all(both, ("row", "core"), 0, 0, tiled=True)
    return pl.pallas_call(
        down_kernel,
        out_shape=jax.ShapeDtypeStruct((vec_count, points), jnp.bfloat16),
        in_specs=[smem, smem] + [vmem] * 6,
        out_specs=vmem,
        compiler_params=params,
        cost_estimate=cost(100_000_000, 3_000_000),
        name="downward",
    )(group_list, group_count, coarse_all, big_all, far, near, transfer, leaf_basis)


def solution(mesh):
    groups, members = mesh.devices.shape
    shape = (groups // 4, 2, 2, deep, members // deep)
    split = Mesh(mesh.devices.reshape(shape), ("row", "half", "core", "deep", "across"))
    group = ("row", "half", "core")
    leaf = ("deep", "across")
    both = group + leaf
    placed = (
        P(None, both),
        P(None, both),
        P(both, None),
        P(both),
        P(both, None, None),
        P(both, None),
        P(both),
        P(both, None, None, None),
        P(both, None, None),
        P(group, None),
        P(group),
        P(group, leaf, None, None),
    )
    return jax.shard_map(body, mesh=split, in_specs=placed, out_specs=P(None, both), check_vma=False)
```

```python
import jax
import jax.numpy as jnp
from jax import lax
from jax.experimental import pallas as pl
from jax.experimental.pallas import tpu as pltpu
from jax.sharding import Mesh
from jax.sharding import PartitionSpec as P

inv_four_pi = 0.07957747154594767
soften = 0.01
sharpness = inv_four_pi**-2
feature_depth = 64
near_at_once = 6
far_at_once = 16
far_shift = 7
id_bits = 5
deep = 4
vmem_bytes = 20 << 20
whole_bytes = 63 << 20

nt_dims = (((1,), (1,)), ((), ()))
nn_dims = (((1,), (0,)), ((), ()))
smem = pl.BlockSpec(memory_space=pltpu.SMEM)
vmem = pl.BlockSpec(memory_space=pltpu.VMEM)
hbm = pl.BlockSpec(memory_space=pltpu.HBM)
params = pltpu.CompilerParams(vmem_limit_bytes=vmem_bytes)
whole = pltpu.CompilerParams(vmem_limit_bytes=whole_bytes)
anywhere = pl.BlockSpec(memory_space=pl.ANY)


def dot(left, right, dims):
    return lax.dot_general(left, right, dims, preferred_element_type=jnp.float32)


def pack(block):
    half = block.shape[0] // 2
    return jnp.concatenate([block[:half], block[half:]], axis=1)


def unpack(block):
    half = block.shape[1] // 2
    return jnp.concatenate([block[:, :half], block[:, half:]], axis=0)


def upward_kernel(
    vec_hbm, off_hbm, basis_hbm, transfer_hbm, group_hbm, halo_ref, big_ref, *scratch
):
    vec_ref, off_ref, basis_ref, transfer_ref, group_ref, sems = scratch
    sources = (vec_hbm, off_hbm, basis_hbm, transfer_hbm, group_hbm)
    copies_in = [
        pltpu.make_async_copy(src, dst, sems.at[i])
        for i, (src, dst) in enumerate(zip(sources, scratch[:5]))
    ]
    for copy in copies_in:
        copy.start()
    vecs, width = vec_ref.shape
    leaves = basis_ref.shape[0]
    points = width // leaves
    copies = big_ref.shape[0]
    rows = vecs // 2
    copies_in[0].wait()
    copies_in[1].wait()
    halo_ref[0:vecs, :] = vec_ref[...]
    halo_ref[vecs : vecs + off_ref.shape[0], :] = off_ref[...]
    for copy in copies_in[2:]:
        copy.wait()
    part = jnp.zeros((vecs, transfer_ref.shape[2]), jnp.float32)
    for i in range(leaves):
        leaf = vec_ref[:, i * points : (i + 1) * points]
        coeff = dot(leaf, basis_ref[i], nt_dims).astype(jnp.bfloat16)
        part = part + dot(coeff, transfer_ref[i], nn_dims)
        packed = pack(coeff)
        for c in range(copies):
            big_ref[c, i * rows : (i + 1) * rows, :] = packed
    coupling = pack(group_ref[0, 0])
    packed_part = pack(part)
    high = packed_part.astype(jnp.bfloat16)
    low = (packed_part - high.astype(jnp.float32)).astype(jnp.bfloat16)
    first = leaves * rows + coupling.shape[0]
    for c in range(copies):
        big_ref[c, leaves * rows : first, :] = coupling
        big_ref[c, first : first + rows, :] = high
        big_ref[c, first + rows :, :] = low


def regroup_kernel(big_ref, out_ref):
    deep, big_rows = big_ref.shape[:2]
    keep = (out_ref.shape[1] - big_rows) // (deep - 1)
    rows = (big_rows - keep) // 2
    total = jnp.zeros((rows, big_ref.shape[2]), jnp.float32)
    for i in range(deep):
        high = big_ref[i, keep : keep + rows, :].astype(jnp.float32)
        total = total + (high + big_ref[i, keep + rows :, :].astype(jnp.float32))
    high = total.astype(jnp.bfloat16)
    low = (total - high.astype(jnp.float32)).astype(jnp.bfloat16)
    for c in range(out_ref.shape[0]):
        for i in range(deep):
            out_ref[c, i * keep : (i + 1) * keep, :] = big_ref[i, :keep, :]
        out_ref[c, deep * keep : deep * keep + rows, :] = high
        out_ref[c, deep * keep + rows :, :] = low


def coarse_kernel(big_ref, near_ref, out_ref):
    members, big_rows = big_ref.shape[:2]
    rows = out_ref.shape[1]
    total = jnp.zeros(out_ref.shape[1:], jnp.float32)
    for i in range(members):
        high = big_ref[i, big_rows - 2 * rows : big_rows - rows, :].astype(jnp.float32)
        total = total + (high + big_ref[i, big_rows - rows :, :].astype(jnp.float32))
    rounded = total.astype(jnp.bfloat16)
    for i in range(out_ref.shape[0]):
        out_ref[i] = rounded


def spread(ids, axis_pos):
    total = jnp.zeros_like(ids)
    for b in range(id_bits):
        bit = jnp.bitwise_and(jnp.right_shift(ids, 3 * b + axis_pos), 1)
        total = total + jnp.left_shift(bit, b)
    return total


def pieces(x):
    first = x.astype(jnp.bfloat16).astype(jnp.float32)
    second = (x - first).astype(jnp.bfloat16).astype(jnp.float32)
    return first, second, (x - first) - second


def near_kernel(
    list_ref, count_ref, own_ref, before_ref, after_ref, first_ref, out_ref, *scratch
):
    source, target, vecs, wide, to_leaf, from_leaf, tiles_a, tiles_b = scratch
    leaves = out_ref.shape[0] - 1
    vec_count, width = out_ref.shape[1:]
    slots = list_ref.shape[1]
    n = leaves * width
    base = list_ref[0, 0]
    rows = lax.broadcasted_iota(jnp.int32, (8, n), 0)
    lanes = lax.broadcasted_iota(jnp.int32, (8, n), 1)
    middle = spread(jnp.full((8, n), base, jnp.int32), rows) + jnp.where(rows == 0, 2, 1)
    wide[...] = jnp.zeros((8, n), jnp.float32)
    blank = jnp.zeros((128 - 56, width), jnp.float32)
    for w, ref in enumerate((before_ref, own_ref, after_ref)):
        for i in range(leaves):
            vecs[w * leaves + i] = ref[0:vec_count, i * width : (i + 1) * width]
        wide[0:3, :] = ref[vec_count : vec_count + 3, :].astype(jnp.float32)
        o = wide[...]
        ids = base + (w - 1) * leaves + jnp.right_shift(lanes, 8)
        c = jnp.where(rows < 3, spread(ids, rows) - middle, 0).astype(jnp.float32)
        p = o + c
        norm = jnp.sum(p * p, axis=0, keepdims=True)
        n1, n2, n3 = pieces(norm * sharpness)
        tail = jnp.where(rows < 6, 1.0, 0.0)
        tail = jnp.where(rows == 0, n1, jnp.where(rows == 1, n2, jnp.where(rows == 2, n3, tail)))
        for i in range(leaves):
            span = slice(i * width, (i + 1) * width)
            o_part, c_part = o[:, span], c[:, span]
            full = jnp.concatenate([o_part] * 3 + [c_part] * 3 + [tail[:, span], blank], axis=0)
            source[w * leaves + i] = jnp.transpose(full).astype(jnp.bfloat16)
        if w == 1:
            t1, t2, t3 = pieces((norm + soften) * sharpness)
            p1, p2, p3 = pieces(p * (-2.0 * sharpness))
            tail = jnp.where(rows == 3, t1, jnp.where(rows == 4, t2, jnp.where(rows == 5, t3, 0.0)))
            tail = jnp.where(rows < 3, 1.0, tail)
            halves = [(p1, p2), (p3, p1), (p2, p3), (tail, jnp.zeros_like(tail))]
            for j, pair in enumerate(halves):
                block = jnp.concatenate(pair, axis=0).astype(jnp.bfloat16)
                for i in range(leaves):
                    target[i, 16 * j : 16 * (j + 1), :] = block[:, i * width : (i + 1) * width]

    def one_leaf(t, q):
        count = count_ref[t]
        for k in range(slots):
            to_leaf[q] = t
            from_leaf[q] = list_ref[t, k] - base + leaves
            q = q + jnp.where(k < count, 1, 0)
        return q

    total = lax.fori_loop(0, leaves, one_leaf, 0)
    for g in range(3 * near_at_once):
        to_leaf[total + g] = leaves
        from_leaf[total + g] = 0
    chunk = 2 * near_at_once
    chunks = lax.div(total + (chunk - 1), chunk)
    out_ref[...] = jnp.zeros_like(out_ref)

    def make_tiles(first, tiles):
        for g in range(near_at_once):
            t = jnp.minimum(to_leaf[first + g], leaves - 1)
            points = source[from_leaf[first + g]][:, :feature_depth]
            tiles[g] = lax.rsqrt(dot(points, target[t], nn_dims)).astype(jnp.bfloat16)

    def use_tiles(first, tiles):
        for g in range(near_at_once):
            out_ref[to_leaf[first + g]] += dot(vecs[from_leaf[first + g]], tiles[g], nn_dims)

    make_tiles(0, tiles_a)

    def step(i, carry):
        first = 2 * near_at_once * i
        make_tiles(first + near_at_once, tiles_b)
        use_tiles(first, tiles_a)
        make_tiles(first + 2 * near_at_once, tiles_a)
        use_tiles(first + near_at_once, tiles_b)
        return carry

    lax.fori_loop(0, chunks, step, 0)


def far_kernel(list_ref, count_ref, big_ref, coupling_ref, first_ref, out_ref, *scratch):
    to_leaf, pair, from_leaf = scratch
    leaves, slots = coupling_ref.shape[:2]
    across = big_ref.shape[0]
    rows = out_ref.shape[1] // 2
    keep = leaves * rows + coupling_ref.shape[2] // 2
    leaf_mask, across_mask = leaves - 1, across - 1
    leaf_shift, across_shift = leaves.bit_length() - 1, across.bit_length() - 1
    slot_shift = slots.bit_length() - 1

    def one_leaf(t, q):
        count = count_ref[t]
        for k in range(slots):
            j = jnp.bitwise_and(list_ref[t, k], across * deep * leaves - 1)
            holder = jnp.right_shift(j, leaf_shift)
            to_leaf[q] = t
            pair[q] = t * slots + k
            place = jnp.right_shift(holder, across_shift) * (keep // rows)
            place = place + jnp.bitwise_and(j, leaf_mask)
            from_leaf[q] = jnp.left_shift(jnp.bitwise_and(holder, across_mask), far_shift) + place
            q = q + jnp.where(k < count, 1, 0)
        return q

    total = lax.fori_loop(0, leaves, one_leaf, 0)
    for g in range(far_at_once):
        to_leaf[total + g] = leaves
        pair[total + g] = 0
        from_leaf[total + g] = 0
    out_ref[...] = jnp.zeros_like(out_ref)

    def step(i, carry):
        terms = []
        for g in range(far_at_once):
            q = i * far_at_once + g
            place = from_leaf[q]
            first = jnp.bitwise_and(place, (1 << far_shift) - 1) * rows
            first = pl.multiple_of(first, rows)
            block = unpack(big_ref[jnp.right_shift(place, far_shift), pl.ds(first, rows), :])
            t, k = jnp.right_shift(pair[q], slot_shift), jnp.bitwise_and(pair[q], slots - 1)
            terms.append(dot(block, coupling_ref[t, k], nt_dims))
        for g, term in enumerate(terms):
            out_ref[to_leaf[i * far_at_once + g]] += term
        return carry

    lax.fori_loop(0, lax.div(total + far_at_once - 1, far_at_once), step, 0)


def down_kernel(
    list_ref, count_ref, coarse_ref, big_ref, far_ref, near_ref, transfer_ref, basis_ref, out_ref
):
    leaves, rank, width = basis_ref.shape
    vec_count = out_ref.shape[0]
    across = big_ref.shape[0]
    rows = vec_count // 2
    keep = leaves * rows + rank // 2
    terms = []
    for k in range(list_ref.shape[1]):
        g = list_ref[0, k]
        low = jnp.bitwise_and(g, 1) * 2 + jnp.bitwise_and(jnp.right_shift(g, 1), 1)
        block = unpack(coarse_ref[low * (coarse_ref.shape[0] // 4) + jnp.right_shift(g, 2)])
        block = jnp.where(k < count_ref[0], block, jnp.zeros_like(block))
        last = (k // across + 1) * keep
        coupling = unpack(big_ref[k % across, last - rank // 2 : last, :])
        terms.append(dot(block, coupling, nt_dims))
    while len(terms) > 1:
        terms = [a + b for a, b in zip(terms[::2], terms[1::2])]
    coarse_out = terms[0].astype(jnp.bfloat16)
    for i in range(leaves):
        local = far_ref[i] + dot(coarse_out, transfer_ref[i], nt_dims)
        result = near_ref[i] + dot(local.astype(jnp.bfloat16), basis_ref[i], nn_dims)
        out_ref[:, i * width : (i + 1) * width] = result.astype(jnp.bfloat16)


def cost(flops, moved, special=0):
    return pl.CostEstimate(flops=flops, bytes_accessed=moved, transcendentals=special)


def body(
    vectors,
    offsets,
    near_list,
    near_count,
    leaf_basis,
    far_list,
    far_count,
    leaf_coupling,
    transfer,
    group_list,
    group_count,
    group_coupling,
):
    across = lax.axis_size("across")
    members = lax.axis_size("deep") * across
    groups = lax.axis_size("row") * 4
    vec_count, points = vectors.shape
    leaves, rank, width = leaf_basis.shape
    rows = vec_count // 2
    keep = leaves * rows + rank // 2
    stacked = vec_count + offsets.shape[0]
    up = [(i, i + 1) for i in range(members - 1)]
    down = [(j, i) for i, j in up]
    inputs = (vectors, offsets, leaf_basis, transfer, group_coupling)
    halo, big = pl.pallas_call(
        upward_kernel,
        out_shape=(
            jax.ShapeDtypeStruct((stacked, points), jnp.bfloat16),
            jax.ShapeDtypeStruct((deep, keep + 2 * rows, 2 * rank), jnp.bfloat16),
        ),
        in_specs=[hbm] * 5,
        out_specs=(vmem, vmem),
        scratch_shapes=[pltpu.VMEM(x.shape, x.dtype) for x in inputs]
        + [pltpu.SemaphoreType.DMA((len(inputs),))],
        compiler_params=whole,
        cost_estimate=cost(40_000_000, 3_000_000),
        name="upward",
    )(*inputs)
    deep_all = lax.all_to_all(big, "deep", 0, 0, tiled=True)
    before = lax.ppermute(halo, ("deep", "across"), up)
    after = lax.ppermute(halo, ("deep", "across"), down)
    wide = pl.pallas_call(
        regroup_kernel,
        out_shape=jax.ShapeDtypeStruct((across, deep * keep + 2 * rows, 2 * rank), jnp.bfloat16),
        in_specs=[vmem],
        out_specs=vmem,
        compiler_params=params,
        cost_estimate=cost(40_000, 2_000_000),
        name="regroup",
    )(deep_all)
    big_all = lax.all_to_all(wide, "across", 0, 0, tiled=True)
    near_pairs = near_list.size + 4 * near_at_once
    far_pairs = far_list.size + 2 * far_at_once
    near = pl.pallas_call(
        near_kernel,
        out_shape=jax.ShapeDtypeStruct((leaves + 1, vec_count, width), jnp.float32),
        in_specs=[smem, smem, vmem, vmem, vmem, anywhere],
        out_specs=vmem,
        scratch_shapes=[
            pltpu.VMEM((3 * leaves, width, 128), jnp.bfloat16),
            pltpu.VMEM((leaves, feature_depth, width), jnp.bfloat16),
            pltpu.VMEM((3 * leaves, vec_count, width), jnp.bfloat16),
            pltpu.VMEM((8, points), jnp.float32),
            pltpu.SMEM((near_pairs,), jnp.int32),
            pltpu.SMEM((near_pairs,), jnp.int32),
            pltpu.VMEM((near_at_once, width, width), jnp.bfloat16),
            pltpu.VMEM((near_at_once, width, width), jnp.bfloat16),
        ],
        compiler_params=params,
        cost_estimate=cost(16_000_000_000, 3_000_000, 15_000_000),
        name="near",
    )(near_list, near_count, halo, before, after, wide)
    coarse = pl.pallas_call(
        coarse_kernel,
        out_shape=jax.ShapeDtypeStruct((groups, rows, 2 * rank), jnp.bfloat16),
        in_specs=[vmem, anywhere],
        out_specs=vmem,
        compiler_params=params,
        cost_estimate=cost(40_000, 300_000),
        name="coarse",
    )(big_all, near)
    coarse_all = lax.all_to_all(coarse, ("core", "half", "row"), 0, 0, tiled=True)
    far = pl.pallas_call(
        far_kernel,
        out_shape=jax.ShapeDtypeStruct((leaves + 1, vec_count, rank), jnp.float32),
        in_specs=[smem, smem, vmem, vmem, anywhere],
        out_specs=vmem,
        scratch_shapes=[pltpu.SMEM((far_pairs,), jnp.int32) for _ in range(3)],
        compiler_params=params,
        cost_estimate=cost(1_000_000_000, 5_000_000),
        name="far",
    )(far_list, far_count, big_all, leaf_coupling, coarse)
    return pl.pallas_call(
        down_kernel,
        out_shape=jax.ShapeDtypeStruct((vec_count, points), jnp.bfloat16),
        in_specs=[smem, smem] + [vmem] * 6,
        out_specs=vmem,
        compiler_params=params,
        cost_estimate=cost(100_000_000, 3_000_000),
        name="downward",
    )(group_list, group_count, coarse_all, big_all, far, near, transfer, leaf_basis)


def solution(mesh):
    groups, members = mesh.devices.shape
    shape = (groups // 4, 2, 2, deep, members // deep)
    split = Mesh(mesh.devices.reshape(shape), ("row", "half", "core", "deep", "across"))
    group = ("row", "half", "core")
    leaf = ("deep", "across")
    both = group + leaf
    placed = (
        P(None, both),
        P(None, both),
        P(both, None),
        P(both),
        P(both, None, None),
        P(both, None),
        P(both),
        P(both, None, None, None),
        P(both, None, None),
        P(group, None),
        P(group),
        P(group, leaf, None, None),
    )
    return jax.shard_map(body, mesh=split, in_specs=placed, out_specs=P(None, both), check_vma=False)
```

```python
import jax
import jax.numpy as jnp
from jax import lax
from jax.experimental import pallas as pl
from jax.experimental.pallas import tpu as pltpu
from jax.sharding import Mesh
from jax.sharding import PartitionSpec as P

inv_four_pi = 0.07957747154594767
soften = 0.01
sharpness = inv_four_pi**-2
feature_depth = 64
near_at_once = 6
far_at_once = 16
far_shift = 7
id_bits = 5
deep = 4
vmem_bytes = 20 << 20
whole_bytes = 63 << 20

nt_dims = (((1,), (1,)), ((), ()))
nn_dims = (((1,), (0,)), ((), ()))
smem = pl.BlockSpec(memory_space=pltpu.SMEM)
vmem = pl.BlockSpec(memory_space=pltpu.VMEM)
hbm = pl.BlockSpec(memory_space=pltpu.HBM)
params = pltpu.CompilerParams(vmem_limit_bytes=vmem_bytes)
whole = pltpu.CompilerParams(vmem_limit_bytes=whole_bytes)
anywhere = pl.BlockSpec(memory_space=pl.ANY)


def dot(left, right, dims):
    return lax.dot_general(left, right, dims, preferred_element_type=jnp.float32)


def pack(block):
    half = block.shape[0] // 2
    return jnp.concatenate([block[:half], block[half:]], axis=1)


def unpack(block):
    half = block.shape[1] // 2
    return jnp.concatenate([block[:, :half], block[:, half:]], axis=0)


def upward_kernel(
    vec_hbm, off_hbm, basis_hbm, transfer_hbm, group_hbm, halo_ref, big_ref, *scratch
):
    vec_ref, off_ref, basis_ref, transfer_ref, group_ref, sems = scratch
    sources = (vec_hbm, off_hbm, basis_hbm, transfer_hbm, group_hbm)
    copies_in = [
        pltpu.make_async_copy(src, dst, sems.at[i])
        for i, (src, dst) in enumerate(zip(sources, scratch[:5]))
    ]
    for copy in copies_in:
        copy.start()
    vecs, width = vec_ref.shape
    leaves = basis_ref.shape[0]
    points = width // leaves
    copies = big_ref.shape[0]
    rows = vecs // 2
    copies_in[0].wait()
    copies_in[1].wait()
    halo_ref[0:vecs, :] = vec_ref[...]
    halo_ref[vecs : vecs + off_ref.shape[0], :] = off_ref[...]
    for copy in copies_in[2:]:
        copy.wait()
    coeffs = []
    for i in range(leaves):
        leaf = vec_ref[:, i * points : (i + 1) * points]
        coeff = dot(leaf, basis_ref[i], nt_dims).astype(jnp.bfloat16)
        coeffs.append(coeff)
        packed = pack(coeff)
        for c in range(copies):
            big_ref[c, i * rows : (i + 1) * rows, :] = packed
    stacked = transfer_ref[...].reshape(leaves * transfer_ref.shape[1], transfer_ref.shape[2])
    part = dot(jnp.concatenate(coeffs, axis=1), stacked, nn_dims)
    coupling = pack(group_ref[0, 0])
    packed_part = pack(part)
    high = packed_part.astype(jnp.bfloat16)
    low = (packed_part - high.astype(jnp.float32)).astype(jnp.bfloat16)
    first = leaves * rows + coupling.shape[0]
    for c in range(copies):
        big_ref[c, leaves * rows : first, :] = coupling
        big_ref[c, first : first + rows, :] = high
        big_ref[c, first + rows :, :] = low


def regroup_kernel(big_ref, out_ref):
    deep, big_rows = big_ref.shape[:2]
    keep = (out_ref.shape[1] - big_rows) // (deep - 1)
    rows = (big_rows - keep) // 2
    total = jnp.zeros((rows, big_ref.shape[2]), jnp.float32)
    for i in range(deep):
        high = big_ref[i, keep : keep + rows, :].astype(jnp.float32)
        total = total + (high + big_ref[i, keep + rows :, :].astype(jnp.float32))
    high = total.astype(jnp.bfloat16)
    low = (total - high.astype(jnp.float32)).astype(jnp.bfloat16)
    for c in range(out_ref.shape[0]):
        for i in range(deep):
            out_ref[c, i * keep : (i + 1) * keep, :] = big_ref[i, :keep, :]
        out_ref[c, deep * keep : deep * keep + rows, :] = high
        out_ref[c, deep * keep + rows :, :] = low


def coarse_kernel(big_ref, near_ref, out_ref):
    members, big_rows = big_ref.shape[:2]
    rows = out_ref.shape[1]
    total = jnp.zeros(out_ref.shape[1:], jnp.float32)
    for i in range(members):
        high = big_ref[i, big_rows - 2 * rows : big_rows - rows, :].astype(jnp.float32)
        total = total + (high + big_ref[i, big_rows - rows :, :].astype(jnp.float32))
    rounded = total.astype(jnp.bfloat16)
    for i in range(out_ref.shape[0]):
        out_ref[i] = rounded


def spread(ids, axis_pos):
    total = jnp.zeros_like(ids)
    for b in range(id_bits):
        bit = jnp.bitwise_and(jnp.right_shift(ids, 3 * b + axis_pos), 1)
        total = total + jnp.left_shift(bit, b)
    return total


def pieces(x):
    first = x.astype(jnp.bfloat16).astype(jnp.float32)
    second = (x - first).astype(jnp.bfloat16).astype(jnp.float32)
    return first, second, (x - first) - second


def near_kernel(
    list_ref, count_ref, own_ref, before_ref, after_ref, first_ref, out_ref, *scratch
):
    source, target, vecs, wide, to_leaf, from_leaf, tiles_a, tiles_b = scratch
    leaves = out_ref.shape[0] - 1
    vec_count, width = out_ref.shape[1:]
    slots = list_ref.shape[1]
    n = leaves * width
    base = list_ref[0, 0]
    rows = lax.broadcasted_iota(jnp.int32, (8, n), 0)
    lanes = lax.broadcasted_iota(jnp.int32, (8, n), 1)
    middle = spread(jnp.full((8, n), base, jnp.int32), rows) + jnp.where(rows == 0, 2, 1)
    wide[...] = jnp.zeros((8, n), jnp.float32)
    blank = jnp.zeros((128 - 56, width), jnp.float32)
    for w, ref in enumerate((before_ref, own_ref, after_ref)):
        for i in range(leaves):
            vecs[w * leaves + i] = ref[0:vec_count, i * width : (i + 1) * width]
        wide[0:3, :] = ref[vec_count : vec_count + 3, :].astype(jnp.float32)
        o = wide[...]
        ids = base + (w - 1) * leaves + jnp.right_shift(lanes, 8)
        c = jnp.where(rows < 3, spread(ids, rows) - middle, 0).astype(jnp.float32)
        p = o + c
        norm = jnp.sum(p * p, axis=0, keepdims=True)
        n1, n2, n3 = pieces(norm * sharpness)
        tail = jnp.where(rows < 6, 1.0, 0.0)
        tail = jnp.where(rows == 0, n1, jnp.where(rows == 1, n2, jnp.where(rows == 2, n3, tail)))
        for i in range(leaves):
            span = slice(i * width, (i + 1) * width)
            o_part, c_part = o[:, span], c[:, span]
            full = jnp.concatenate([o_part] * 3 + [c_part] * 3 + [tail[:, span], blank], axis=0)
            source[w * leaves + i] = jnp.transpose(full).astype(jnp.bfloat16)
        if w == 1:
            t1, t2, t3 = pieces((norm + soften) * sharpness)
            p1, p2, p3 = pieces(p * (-2.0 * sharpness))
            tail = jnp.where(rows == 3, t1, jnp.where(rows == 4, t2, jnp.where(rows == 5, t3, 0.0)))
            tail = jnp.where(rows < 3, 1.0, tail)
            halves = [(p1, p2), (p3, p1), (p2, p3), (tail, jnp.zeros_like(tail))]
            for j, pair in enumerate(halves):
                block = jnp.concatenate(pair, axis=0).astype(jnp.bfloat16)
                for i in range(leaves):
                    target[i, 16 * j : 16 * (j + 1), :] = block[:, i * width : (i + 1) * width]

    def one_leaf(t, q):
        count = count_ref[t]
        for k in range(slots):
            to_leaf[q] = t
            from_leaf[q] = list_ref[t, k] - base + leaves
            q = q + jnp.where(k < count, 1, 0)
        return q

    total = lax.fori_loop(0, leaves, one_leaf, 0)
    for g in range(3 * near_at_once):
        to_leaf[total + g] = leaves
        from_leaf[total + g] = 0
    chunk = 2 * near_at_once
    chunks = lax.div(total + (chunk - 1), chunk)
    out_ref[...] = jnp.zeros_like(out_ref)

    def make_tiles(first, tiles):
        for g in range(near_at_once):
            t = jnp.minimum(to_leaf[first + g], leaves - 1)
            points = source[from_leaf[first + g]][:, :feature_depth]
            tiles[g] = lax.rsqrt(dot(points, target[t], nn_dims)).astype(jnp.bfloat16)

    def use_tiles(first, tiles):
        for g in range(near_at_once):
            out_ref[to_leaf[first + g]] += dot(vecs[from_leaf[first + g]], tiles[g], nn_dims)

    make_tiles(0, tiles_a)

    def step(i, carry):
        first = 2 * near_at_once * i
        make_tiles(first + near_at_once, tiles_b)
        use_tiles(first, tiles_a)
        make_tiles(first + 2 * near_at_once, tiles_a)
        use_tiles(first + near_at_once, tiles_b)
        return carry

    lax.fori_loop(0, chunks, step, 0)


def far_kernel(list_ref, count_ref, big_ref, coupling_ref, first_ref, out_ref, *scratch):
    to_leaf, pair, from_leaf = scratch
    leaves, slots = coupling_ref.shape[:2]
    across = big_ref.shape[0]
    rows = out_ref.shape[1] // 2
    keep = leaves * rows + coupling_ref.shape[2] // 2
    leaf_mask, across_mask = leaves - 1, across - 1
    leaf_shift, across_shift = leaves.bit_length() - 1, across.bit_length() - 1
    slot_shift = slots.bit_length() - 1

    def one_leaf(t, q):
        count = count_ref[t]
        for k in range(slots):
            j = jnp.bitwise_and(list_ref[t, k], across * deep * leaves - 1)
            holder = jnp.right_shift(j, leaf_shift)
            to_leaf[q] = t
            pair[q] = t * slots + k
            place = jnp.right_shift(holder, across_shift) * (keep // rows)
            place = place + jnp.bitwise_and(j, leaf_mask)
            from_leaf[q] = jnp.left_shift(jnp.bitwise_and(holder, across_mask), far_shift) + place
            q = q + jnp.where(k < count, 1, 0)
        return q

    total = lax.fori_loop(0, leaves, one_leaf, 0)
    for g in range(far_at_once):
        to_leaf[total + g] = leaves
        pair[total + g] = 0
        from_leaf[total + g] = 0
    out_ref[...] = jnp.zeros_like(out_ref)

    def step(i, carry):
        terms = []
        for g in range(far_at_once):
            q = i * far_at_once + g
            place = from_leaf[q]
            first = jnp.bitwise_and(place, (1 << far_shift) - 1) * rows
            first = pl.multiple_of(first, rows)
            block = unpack(big_ref[jnp.right_shift(place, far_shift), pl.ds(first, rows), :])
            t, k = jnp.right_shift(pair[q], slot_shift), jnp.bitwise_and(pair[q], slots - 1)
            terms.append(dot(block, coupling_ref[t, k], nt_dims))
        for g, term in enumerate(terms):
            out_ref[to_leaf[i * far_at_once + g]] += term
        return carry

    lax.fori_loop(0, lax.div(total + far_at_once - 1, far_at_once), step, 0)


def down_kernel(
    list_ref, count_ref, coarse_ref, big_ref, far_ref, near_ref, transfer_ref, basis_ref, out_ref
):
    leaves, rank, width = basis_ref.shape
    vec_count = out_ref.shape[0]
    across = big_ref.shape[0]
    rows = vec_count // 2
    keep = leaves * rows + rank // 2
    terms = []
    for k in range(list_ref.shape[1]):
        g = list_ref[0, k]
        low = jnp.bitwise_and(g, 1) * 2 + jnp.bitwise_and(jnp.right_shift(g, 1), 1)
        block = unpack(coarse_ref[low * (coarse_ref.shape[0] // 4) + jnp.right_shift(g, 2)])
        block = jnp.where(k < count_ref[0], block, jnp.zeros_like(block))
        last = (k // across + 1) * keep
        coupling = unpack(big_ref[k % across, last - rank // 2 : last, :])
        terms.append(dot(block, coupling, nt_dims))
    while len(terms) > 1:
        terms = [a + b for a, b in zip(terms[::2], terms[1::2])]
    coarse_out = terms[0].astype(jnp.bfloat16)
    stacked = transfer_ref[...].reshape(leaves * rank, transfer_ref.shape[2])
    downward = dot(coarse_out, stacked, nt_dims)
    for i in range(leaves):
        local = far_ref[i] + downward[:, i * rank : (i + 1) * rank]
        result = near_ref[i] + dot(local.astype(jnp.bfloat16), basis_ref[i], nn_dims)
        out_ref[:, i * width : (i + 1) * width] = result.astype(jnp.bfloat16)


def cost(flops, moved, special=0):
    return pl.CostEstimate(flops=flops, bytes_accessed=moved, transcendentals=special)


def body(
    vectors,
    offsets,
    near_list,
    near_count,
    leaf_basis,
    far_list,
    far_count,
    leaf_coupling,
    transfer,
    group_list,
    group_count,
    group_coupling,
):
    across = lax.axis_size("across")
    members = lax.axis_size("deep") * across
    groups = lax.axis_size("row") * 4
    vec_count, points = vectors.shape
    leaves, rank, width = leaf_basis.shape
    rows = vec_count // 2
    keep = leaves * rows + rank // 2
    stacked = vec_count + offsets.shape[0]
    up = [(i, i + 1) for i in range(members - 1)]
    down = [(j, i) for i, j in up]
    inputs = (vectors, offsets, leaf_basis, transfer, group_coupling)
    halo, big = pl.pallas_call(
        upward_kernel,
        out_shape=(
            jax.ShapeDtypeStruct((stacked, points), jnp.bfloat16),
            jax.ShapeDtypeStruct((deep, keep + 2 * rows, 2 * rank), jnp.bfloat16),
        ),
        in_specs=[hbm] * 5,
        out_specs=(vmem, vmem),
        scratch_shapes=[pltpu.VMEM(x.shape, x.dtype) for x in inputs]
        + [pltpu.SemaphoreType.DMA((len(inputs),))],
        compiler_params=whole,
        cost_estimate=cost(40_000_000, 3_000_000),
        name="upward",
    )(*inputs)
    deep_all = lax.all_to_all(big, "deep", 0, 0, tiled=True)
    before = lax.ppermute(halo, ("deep", "across"), up)
    after = lax.ppermute(halo, ("deep", "across"), down)
    wide = pl.pallas_call(
        regroup_kernel,
        out_shape=jax.ShapeDtypeStruct((across, deep * keep + 2 * rows, 2 * rank), jnp.bfloat16),
        in_specs=[vmem],
        out_specs=vmem,
        compiler_params=params,
        cost_estimate=cost(40_000, 2_000_000),
        name="regroup",
    )(deep_all)
    big_all = lax.all_to_all(wide, "across", 0, 0, tiled=True)
    near_pairs = near_list.size + 4 * near_at_once
    far_pairs = far_list.size + 2 * far_at_once
    near = pl.pallas_call(
        near_kernel,
        out_shape=jax.ShapeDtypeStruct((leaves + 1, vec_count, width), jnp.float32),
        in_specs=[smem, smem, vmem, vmem, vmem, anywhere],
        out_specs=vmem,
        scratch_shapes=[
            pltpu.VMEM((3 * leaves, width, 128), jnp.bfloat16),
            pltpu.VMEM((leaves, feature_depth, width), jnp.bfloat16),
            pltpu.VMEM((3 * leaves, vec_count, width), jnp.bfloat16),
            pltpu.VMEM((8, points), jnp.float32),
            pltpu.SMEM((near_pairs,), jnp.int32),
            pltpu.SMEM((near_pairs,), jnp.int32),
            pltpu.VMEM((near_at_once, width, width), jnp.bfloat16),
            pltpu.VMEM((near_at_once, width, width), jnp.bfloat16),
        ],
        compiler_params=params,
        cost_estimate=cost(16_000_000_000, 3_000_000, 15_000_000),
        name="near",
    )(near_list, near_count, halo, before, after, wide)
    coarse = pl.pallas_call(
        coarse_kernel,
        out_shape=jax.ShapeDtypeStruct((groups, rows, 2 * rank), jnp.bfloat16),
        in_specs=[vmem, anywhere],
        out_specs=vmem,
        compiler_params=params,
        cost_estimate=cost(40_000, 300_000),
        name="coarse",
    )(big_all, near)
    coarse_all = lax.all_to_all(coarse, ("core", "half", "row"), 0, 0, tiled=True)
    far = pl.pallas_call(
        far_kernel,
        out_shape=jax.ShapeDtypeStruct((leaves + 1, vec_count, rank), jnp.float32),
        in_specs=[smem, smem, vmem, vmem, anywhere],
        out_specs=vmem,
        scratch_shapes=[pltpu.SMEM((far_pairs,), jnp.int32) for _ in range(3)],
        compiler_params=params,
        cost_estimate=cost(1_000_000_000, 5_000_000),
        name="far",
    )(far_list, far_count, big_all, leaf_coupling, coarse)
    return pl.pallas_call(
        down_kernel,
        out_shape=jax.ShapeDtypeStruct((vec_count, points), jnp.bfloat16),
        in_specs=[smem, smem] + [vmem] * 6,
        out_specs=vmem,
        compiler_params=params,
        cost_estimate=cost(100_000_000, 3_000_000),
        name="downward",
    )(group_list, group_count, coarse_all, big_all, far, near, transfer, leaf_basis)


def solution(mesh):
    groups, members = mesh.devices.shape
    shape = (groups // 4, 2, 2, deep, members // deep)
    split = Mesh(mesh.devices.reshape(shape), ("row", "half", "core", "deep", "across"))
    group = ("row", "half", "core")
    leaf = ("deep", "across")
    both = group + leaf
    placed = (
        P(None, both),
        P(None, both),
        P(both, None),
        P(both),
        P(both, None, None),
        P(both, None),
        P(both),
        P(both, None, None, None),
        P(both, None, None),
        P(group, None),
        P(group),
        P(group, leaf, None, None),
    )
    return jax.shard_map(body, mesh=split, in_specs=placed, out_specs=P(None, both), check_vma=False)
```
